512 devices in a mesh: ctx: 64 (over z, x, core), head: 8 (over y).
Axes of the slice: x: 4, y: 8, z: 8, core: 2. Of those that a mesh axis runs over, the one named last changes fastest.
Arguments:
- queries: bfloat16 [16384, 5120], P('ctx', 'head'), may hold values from -6 to 6
- keys: bfloat16 [16384, 5120], P('ctx', 'head'), may hold values from -6 to 6
- values: bfloat16 [16384, 5120], P('ctx', 'head'), may hold values from -21 to 21
- out_grad: bfloat16 [16384, 5120], P('ctx', 'head'), may hold values from -6 to 6
- rates: float32 [40], P('head'), may hold values from 6.1035156e-06 to 0.08
- gain: float32 [5120], P('head'), may hold values from 0.5 to 1.5
Outputs:
- query_grad: bfloat16 [16384, 5120], P('ctx', 'head')
- key_grad: bfloat16 [16384, 5120], P('ctx', 'head')
- value_grad: bfloat16 [16384, 5120], P('ctx', 'head')
The draws below stay inside these ranges and needn't reach their ends.
All inputs are finite; a program needn't handle non-finite values.
Results may differ from the reference program's by a relative error of at most 0.0069.
Values sent between devices are 32-bit elements; how exact they have to be, the bound alone decides.
No kernel may reach another device: no remote copies, remote signals or barrier semaphores. Data moves between devices by JAX's collectives and lax.ppermute only.
A program may use at most 128 MiB of HBM per device.

```python
import jax
import jax.numpy as jnp
from jax import lax

HD = 128
HEADS = 40
BLOCK = 256
TOKENS = 16384


def draw_values(key, part):
    first = jax.random.fold_in(jax.random.fold_in(key, 11), 0)
    rising = 3.0 ** (jnp.arange(HEADS, dtype=jnp.float32) / max(HEADS - 1, 1))
    base = jnp.clip(jax.random.normal(first, (TOKENS, HEADS, HD), jnp.float32), -6.0, 6.0)
    return (base * rising[None, :, None]).reshape(TOKENS, HEADS * HD).astype(jnp.bfloat16)


def draw_rates(key, part):
    first, second = jax.random.split(jax.random.fold_in(key, 23))
    spread = jax.random.uniform(first, (HEADS,), jnp.float32)
    picker = jax.random.uniform(second, (HEADS,), jnp.float32)
    slow = jnp.exp(jnp.log(0.1 / TOKENS) + spread * jnp.log(23.0))
    fast = jnp.exp(jnp.log(2.3 / TOKENS) + spread * jnp.log(0.08 * TOKENS / 2.3))
    share = 0.55
    return jnp.where(picker < share, slow, fast).astype(jnp.float32)


def steps_of(key, dims, pieces, least, high):
    level, own = 1.0, jax.random.fold_in(key, 6)
    for position, parts in pieces:
        draws = jnp.exp(jax.random.uniform(jax.random.fold_in(own, position), (parts,), jnp.float32, least / len(pieces), high / len(pieces)))
        level = level * jnp.repeat(draws, dims[position] // parts).reshape([-1 if axis == position else 1 for axis in range(len(dims))])
    return level


def noise(key, extent, scale, most, pieces=(), kind=jnp.bfloat16):
    factor_of = steps_of(key, extent, pieces, -0.22, 0.18) if pieces else 1.0
    drawn = jax.random.normal(key, extent, jnp.float32) * scale * factor_of
    return jnp.minimum(jnp.maximum(drawn, -most), most).astype(kind)


def setup_inputs(seed: int = 0) -> dict:
    key_of = jax.random.split(jax.random.key(seed), 7)
    queries = noise(key_of[0], (TOKENS, HEADS * HD), 1.0, 6.0, ((0, 64), (1, 8)))
    keys = noise(key_of[1], (TOKENS, HEADS * HD), 1.0, 6.0, ((0, 64), (1, 8)))
    values = draw_values(jax.random.fold_in(key_of[6], 71), 0)
    out_grad = noise(key_of[3], (TOKENS, HEADS * HD), 1.0, 6.0, ((0, 64), (1, 8)))
    rates = draw_rates(jax.random.fold_in(key_of[6], 71), 0)
    gain = jnp.clip(1.0 + 0.1 * jax.random.normal(key_of[5], (HEADS * HD,), jnp.float32), 0.5, 1.5)
    return {"queries": queries, "keys": keys, "values": values, "out_grad": out_grad, "rates": rates, "gain": gain}


epsilon = 1e-05

def round_trip(value):
    return lax.optimization_barrier(value.astype(jnp.bfloat16)).astype(jnp.float32)

def decay_tables(rates):
    places = jnp.arange(BLOCK, dtype=jnp.float32)
    decay_in = jnp.exp(-rates[None, :] * (places[:, None] + 1.0))
    decay_out = jnp.exp(-rates[None, :] * (BLOCK - 1.0 - places)[:, None])
    offsets = places[:, None] - places[None, :]
    decay_mask = jnp.where(offsets[None] >= 0.0, jnp.exp(-rates[:, None, None] * jnp.maximum(offsets, 0.0)[None]), 0.0)
    block_decay = jnp.exp(-rates * BLOCK)
    return (decay_in, decay_out, decay_mask, block_decay)

def reference(queries, keys, values, out_grad, rates, gain):
    block_count = TOKENS // BLOCK
    shape_four = (block_count, BLOCK, HEADS, HD)
    query_all = queries.reshape(shape_four).astype(jnp.float32)
    key_all = keys.reshape(shape_four).astype(jnp.float32)
    value_all = values.reshape(shape_four).astype(jnp.float32)
    decay_in, decay_out, decay_mask, block_decay = decay_tables(rates)

    def forward_step(state, block):
        query_block, key_block, value_block = block
        attn = round_trip(jnp.einsum('ihd,jhd->hij', query_block, key_block) * decay_mask)
        query_dec = round_trip(query_block * decay_in[:, :, None])
        key_dec = round_trip(key_block * decay_out[:, :, None])
        held = round_trip(state)
        result = jnp.einsum('hij,jhe->ihe', attn, value_block) + jnp.einsum('ihd,hde->ihe', query_dec, held)
        state = block_decay[:, None, None] * state + jnp.einsum('jhd,jhe->hde', key_dec, value_block)
        return (state, (result, held))
    start = jnp.zeros((HEADS, HD, HD), jnp.float32)
    unused, (attn_out, held_all) = lax.scan(forward_step, start, (query_all, key_all, value_all))
    square_sum = lax.optimization_barrier(jnp.sum(attn_out * attn_out, axis=(2, 3)))
    inverse_norm = lax.rsqrt(square_sum / (HEADS * HD) + epsilon)[:, :, None, None]
    weighted = out_grad.reshape(shape_four).astype(jnp.float32) * gain.reshape(HEADS, HD)
    cross = lax.optimization_barrier(jnp.sum(weighted * attn_out, axis=(2, 3)))[:, :, None, None]
    d_out = round_trip(weighted * inverse_norm - attn_out * inverse_norm ** 3 * cross / (HEADS * HD))

    def backward_step(state, block):
        query_block, key_block, value_block, grad_block, held = block
        attn = round_trip(jnp.einsum('ihd,jhd->hij', query_block, key_block) * decay_mask)
        back_attn = round_trip(jnp.einsum('ihe,jhe->hij', grad_block, value_block) * decay_mask)
        query_dec = round_trip(query_block * decay_in[:, :, None])
        key_dec = round_trip(key_block * decay_out[:, :, None])
        value_dec = round_trip(value_block * decay_out[:, :, None])
        later = round_trip(state)
        grad_dec = round_trip(grad_block * decay_in[:, :, None])
        query_grad = jnp.einsum('hij,jhd->ihd', back_attn, key_block) + jnp.einsum('ihe,hde->ihd', grad_dec, held)
        key_grad = jnp.einsum('hij,ihd->jhd', back_attn, query_block) + jnp.einsum('jhe,hde->jhd', value_dec, later)
        value_grad = jnp.einsum('hij,ihe->jhe', attn, grad_block) + jnp.einsum('jhd,hde->jhe', key_dec, later)
        state = block_decay[:, None, None] * state + jnp.einsum('ihd,ihe->hde', query_dec, grad_block)
        return (state, (query_grad.astype(jnp.bfloat16), key_grad.astype(jnp.bfloat16), value_grad.astype(jnp.bfloat16)))
    unused, (query_grad, key_grad, value_grad) = lax.scan(backward_step, start, (query_all, key_all, value_all, d_out, held_all), reverse=True)
    flat = (TOKENS, HEADS * HD)
    return (query_grad.reshape(flat), key_grad.reshape(flat), value_grad.reshape(flat))
```

```python
import jax
import jax.numpy as jnp
from jax import lax
from jax.experimental import pallas as pl
from jax.experimental.pallas import tpu as pltpu
from jax.sharding import PartitionSpec as P

HD = 128
HEADS = 40
BLOCK = 256
epsilon = 1e-05

F32 = jnp.float32
BF16 = jnp.bfloat16
VMEM = pl.BlockSpec(memory_space=pltpu.VMEM)
SMEM = pl.BlockSpec(memory_space=pltpu.SMEM)


def dot(a, b, ca, cb):
    return lax.dot_general(a, b, (((ca,), (cb,)), ((), ())), preferred_element_type=F32)


def head(ref, h):
    return ref[:, h * HD:(h + 1) * HD]


def decay_in_of(rate):
    place = lax.broadcasted_iota(jnp.int32, (BLOCK, HD), 0).astype(F32)
    return jnp.exp(-rate * (place + 1.0))


def decay_out_of(rate):
    place = lax.broadcasted_iota(jnp.int32, (BLOCK, HD), 0).astype(F32)
    return jnp.exp(-rate * (BLOCK - 1.0 - place))


def mask_of(rate):
    row = lax.broadcasted_iota(jnp.int32, (BLOCK, BLOCK), 0)
    col = lax.broadcasted_iota(jnp.int32, (BLOCK, BLOCK), 1)
    offset = (row - col).astype(F32)
    return jnp.where(offset >= 0.0, jnp.exp(-rate * jnp.maximum(offset, 0.0)), 0.0)


def scaled(ref, h, scale):
    return (head(ref, h).astype(F32) * scale).astype(BF16)


def put_state(ref, h, state):
    halves, chips, width = ref.shape
    share = HD // halves // chips
    for half in range(halves):
        for r in range(share):
            lane = (h * share + r) * HD
            row = half * (HD // halves) + r * chips
            ref[half, :, lane:lane + HD] = state[row:row + chips, :]


def get_state(ref, h):
    halves, chips, width = ref.shape
    share = HD // halves // chips
    rows = []
    for half in range(halves):
        for r in range(share):
            lane = (h * share + r) * HD
            rows.append(ref[half, :, lane:lane + HD])
    return jnp.concatenate(rows, axis=0).astype(BF16)


def kv_kernel(rates, keys, values, terms):
    for h in range(rates.shape[0]):
        key_dec = scaled(keys, h, decay_out_of(rates[h]))
        put_state(terms, h, dot(key_dec, head(values, h), 0, 0))


def intra_kernel(rates, queries, keys, values, attn, intra):
    for h in range(rates.shape[0]):
        scores = dot(head(queries, h), head(keys, h), 1, 1)
        weights = (scores * mask_of(rates[h])).astype(BF16)
        attn[h] = weights
        intra[:, h * HD:(h + 1) * HD] = dot(weights, head(values, h), 1, 0)


def join_kernel(backward, rates, pair, total):
    count = rates.shape[0]
    wide = total.shape[1] // count
    for h in range(count):
        lanes = slice(h * wide, (h + 1) * wide)
        decay = jnp.exp(jnp.full((1, wide), -rates[h] * BLOCK, F32))
        first, second = pair[0, :, lanes], pair[1, :, lanes]
        total[:, lanes] = first + decay * second if backward else decay * first + second


def scan_kernel(backward, rates, totals, prefix):
    count = rates.shape[0]
    chips, width = totals.shape
    wide = width // count
    row = lax.broadcasted_iota(jnp.int32, (chips, chips), 0)
    col = lax.broadcasted_iota(jnp.int32, (chips, chips), 1)
    gap = (col - row - 1) if backward else (row - col - 1)
    far = gap.astype(F32)
    for h in range(count):
        lanes = slice(h * wide, (h + 1) * wide)
        weight = jnp.where(far >= 0.0, jnp.exp(-(rates[h] * (2.0 * BLOCK)) * jnp.maximum(far, 0.0)), 0.0)
        prefix[:, lanes] = lax.dot_general(
            weight, totals[:, lanes], (((1,), (0,)), ((), ())),
            precision=lax.Precision.HIGHEST, preferred_element_type=F32)


def spread_kernel(backward, rates, prefix, pair, states):
    count = rates.shape[0]
    wide = prefix.shape[1] // count
    near, far = (1, 0) if backward else (0, 1)
    for h in range(count):
        lanes = slice(h * wide, (h + 1) * wide)
        decay = jnp.exp(jnp.full((1, wide), -rates[h] * BLOCK, F32))
        incoming = prefix[:, lanes]
        states[near, :, lanes] = incoming
        states[far, :, lanes] = decay * incoming + pair[near, :, lanes]


def out_kernel(rates, queries, out_grad, gain, intra, states, out, held, sums):
    square = jnp.zeros((BLOCK, HD), F32)
    cross = jnp.zeros((BLOCK, HD), F32)
    for h in range(rates.shape[0]):
        lanes = slice(h * HD, (h + 1) * HD)
        state = get_state(states, h)
        held[:, lanes] = state
        query_dec = scaled(queries, h, decay_in_of(rates[h]))
        result = intra[:, lanes] + dot(query_dec, state, 1, 0)
        out[:, lanes] = result
        weighted = head(out_grad, h).astype(F32) * gain[:, lanes]
        square = square + result * result
        cross = cross + weighted * result
    square = jnp.sum(square.T, axis=0, keepdims=True)
    cross = jnp.sum(cross.T, axis=0, keepdims=True)
    both = jnp.concatenate([square, cross], axis=0)
    for peer in range(sums.shape[0]):
        sums[peer] = both


def grad_kernel(rates, queries, out_grad, gain, out, sums, d_out, terms):
    total = jnp.sum(sums[...], axis=0)
    inverse = lax.rsqrt(total[0:1] / (HEADS * HD) + epsilon)
    factor = inverse * inverse * inverse * total[1:2] / (HEADS * HD)
    inverse = jnp.broadcast_to(inverse, (HD, BLOCK)).T
    factor = jnp.broadcast_to(factor, (HD, BLOCK)).T
    for h in range(rates.shape[0]):
        lanes = slice(h * HD, (h + 1) * HD)
        weighted = head(out_grad, h).astype(F32) * gain[:, lanes]
        grad = (weighted * inverse - out[:, lanes] * factor).astype(BF16)
        d_out[:, lanes] = grad
        query_dec = scaled(queries, h, decay_in_of(rates[h]))
        put_state(terms, h, dot(query_dec, grad, 0, 0))


def local_kernel(rates, queries, keys, values, attn, d_out, held, query_grad, key_part, value_part):
    for h in range(rates.shape[0]):
        lanes = slice(h * HD, (h + 1) * HD)
        grad = head(d_out, h)
        back = (dot(grad, head(values, h), 1, 1) * mask_of(rates[h])).astype(BF16)
        grad_dec = (grad.astype(F32) * decay_in_of(rates[h])).astype(BF16)
        query_grad[:, lanes] = (
            dot(back, head(keys, h), 1, 0) + dot(grad_dec, head(held, h), 1, 1)).astype(BF16)
        key_part[:, lanes] = dot(back, head(queries, h), 0, 0)
        value_part[:, lanes] = dot(attn[h], grad, 0, 0)


def last_kernel(rates, keys, values, states, key_part, value_part, key_grad, value_grad):
    for h in range(rates.shape[0]):
        lanes = slice(h * HD, (h + 1) * HD)
        later = get_state(states, h)
        decay_out = decay_out_of(rates[h])
        value_dec = scaled(values, h, decay_out)
        key_dec = scaled(keys, h, decay_out)
        key_grad[:, lanes] = (key_part[:, lanes] + dot(value_dec, later, 1, 1)).astype(BF16)
        value_grad[:, lanes] = (value_part[:, lanes] + dot(key_dec, later, 1, 0)).astype(BF16)


def call(body, name, rates, args, shapes, flops=0):
    outs = [jax.ShapeDtypeStruct(shape, kind) for shape, kind in shapes]
    moved = sum(a.size * a.dtype.itemsize for a in args)
    return pl.pallas_call(
        body,
        out_shape=outs if len(outs) > 1 else outs[0],
        in_specs=[SMEM] + [VMEM] * len(args),
        out_specs=[VMEM] * len(outs) if len(outs) > 1 else VMEM,
        compiler_params=pltpu.CompilerParams(vmem_limit_bytes=24 * 1024 * 1024),
        cost_estimate=pl.CostEstimate(flops=flops, bytes_accessed=moved, transcendentals=0),
        name=name,
    )(rates, *args)


def swap(array, groups):
    return lax.all_to_all(array, "ctx", 0, 0, tiled=True, axis_index_groups=groups)


def scan(terms, rates, chips, backward):
    pairs = [[2 * i, 2 * i + 1] for i in range(chips)]
    rings = [[2 * i + c for i in range(chips)] for c in range(2)]
    width = terms.shape[2]

    def bound(body):
        return lambda *refs: body(backward, *refs)

    pair = swap(terms, pairs)
    total = call(bound(join_kernel), "join", rates, [pair], [((chips, width), F32)])
    total = swap(total, rings)
    prefix = call(bound(scan_kernel), "scan", rates, [total], [((chips, width), F32)])
    prefix = swap(prefix, rings)
    states = call(bound(spread_kernel), "spread", rates, [prefix, pair], [((2, chips, width), F32)])
    return swap(states, pairs)


def per_device(queries, keys, values, out_grad, rates, gain):
    tokens, width = queries.shape
    count = rates.shape[0]
    chips = lax.axis_size("ctx") // 2
    ranks = lax.axis_size("head")
    state_shape = (2, chips, count * HD * HD // 2 // chips)
    gain = gain.reshape(1, width)

    terms = call(kv_kernel, "kv", rates, [keys, values], [(state_shape, F32)])
    attn, intra = call(
        intra_kernel, "intra", rates, [queries, keys, values],
        [((count, BLOCK, BLOCK), BF16), ((BLOCK, width), F32)], 4 * BLOCK * BLOCK * width)
    states = scan(terms, rates, chips, False)
    out, held, sums = call(
        out_kernel, "out", rates, [queries, out_grad, gain, intra, states],
        [((BLOCK, width), F32), ((HD, width), BF16), ((ranks, 2, BLOCK), F32)])
    sums = lax.all_to_all(sums, "head", 0, 0, tiled=True)
    d_out, terms = call(
        grad_kernel, "grad", rates, [queries, out_grad, gain, out, sums],
        [((BLOCK, width), BF16), (state_shape, F32)])
    query_grad, key_part, value_part = call(
        local_kernel, "local", rates, [queries, keys, values, attn, d_out, held],
        [((BLOCK, width), BF16), ((BLOCK, width), F32), ((BLOCK, width), F32)], 8 * BLOCK * BLOCK * width)
    states = scan(terms, rates, chips, True)
    key_grad, value_grad = call(
        last_kernel, "last", rates, [keys, values, states, key_part, value_part],
        [((BLOCK, width), BF16), ((BLOCK, width), BF16)])
    return query_grad, key_grad, value_grad


def solution(mesh):
    spec = P("ctx", "head")
    return jax.shard_map(
        per_device, mesh=mesh, in_specs=(spec, spec, spec, spec, P("head"), P("head")),
        out_specs=(spec, spec, spec), check_vma=False)
```

```python
import functools

import jax
import jax.numpy as jnp
from jax import lax
from jax.experimental import pallas as pl
from jax.experimental.pallas import tpu as pltpu
from jax.sharding import PartitionSpec as P

HD = 128
HEADS = 40
BLOCK = 256
epsilon = 1e-05

F32 = jnp.float32
BF16 = jnp.bfloat16
VMEM = pl.BlockSpec(memory_space=pltpu.VMEM)
HBM = pl.BlockSpec(memory_space=pltpu.HBM)


def dot(a, b, ca, cb):
    return lax.dot_general(a, b, (((ca,), (cb,)), ((), ())), preferred_element_type=F32)


def lanes_of(h):
    return slice(h * HD, (h + 1) * HD)


def head(ref, h):
    return ref[:, lanes_of(h)]


def decay_in_of(rate):
    place = lax.broadcasted_iota(jnp.int32, (BLOCK, HD), 0).astype(F32)
    return jnp.exp(-rate * (place + 1.0))


def decay_out_of(rate):
    place = lax.broadcasted_iota(jnp.int32, (BLOCK, HD), 0).astype(F32)
    return jnp.exp(-rate * (BLOCK - 1.0 - place))


def mask_of(rate):
    row = lax.broadcasted_iota(jnp.int32, (BLOCK, BLOCK), 0)
    col = lax.broadcasted_iota(jnp.int32, (BLOCK, BLOCK), 1)
    offset = (row - col).astype(F32)
    return jnp.where(offset >= 0.0, jnp.exp(-rate * jnp.maximum(offset, 0.0)), 0.0)


def short(rows, h):
    return rows[h:h + 1, 0:HD]


def scaled(array, scale):
    return (array.astype(F32) * scale).astype(BF16)


def put_halves(keep, send, h, state, odd):
    chips = keep.shape[0]
    share = HD // 2 // chips
    low, high = state[:HD // 2], state[HD // 2:]
    mine, other = jnp.where(odd, high, low), jnp.where(odd, low, high)
    for r in range(share):
        lane = (h * share + r) * HD
        keep[:, lane:lane + HD] = mine[r * chips:(r + 1) * chips]
        send[:, lane:lane + HD] = other[r * chips:(r + 1) * chips]


def get_half(ref, h):
    chips = ref.shape[0]
    share = HD // 2 // chips
    return jnp.concatenate([ref[:, lanes_of(h * share + r)] for r in range(share)], axis=0)


def get_state(mine, other, h, odd):
    mine, other = get_half(mine, h), get_half(other, h)
    low, high = jnp.where(odd, other, mine), jnp.where(odd, mine, other)
    return jnp.concatenate([low, high], axis=0).astype(BF16)


def kv_kernel(rates, keys, values, keep, send, rows, mixing, rate, key_in, value_in, sems):
    count = rates.shape[0]
    odd = lax.rem(lax.axis_index("ctx"), 2) == 1
    copies = [pltpu.make_async_copy(rates, rate, sems.at[2 * count])]
    for h in range(count):
        for which, (source, target) in enumerate(((keys, key_in), (values, value_in))):
            copies.append(pltpu.make_async_copy(
                source.at[:, lanes_of(h)], target.at[:, lanes_of(h)], sems.at[2 * h + which]))
    for copy in copies:
        copy.start()
    copies[0].wait()
    wide = mixing.shape[1] // count
    first_rows = lax.broadcasted_iota(jnp.int32, (8, wide), 0)
    for h in range(count):
        rows[h:h + 1, :] = jnp.full((1, BLOCK), rate[h], F32)
        decay = jnp.exp(jnp.full((8, wide), -rate[h] * BLOCK, F32))
        place = lax.rem(first_rows, 4)
        later = first_rows >= 4
        first = later == odd
        on_first = jnp.where(place == 0, decay, jnp.where(place == 2, 0.0, 1.0))
        on_second = jnp.where(place == 1, decay, jnp.where(place == 3, 0.0, 1.0))
        mixing[:, h * wide:(h + 1) * wide] = jnp.where(first, on_first, on_second)
    for h in range(count):
        decay_out = decay_out_of(rate[h])
        copies[1 + 2 * h].wait()
        copies[2 + 2 * h].wait()
        key_dec = scaled(head(key_in, h), decay_out)
        put_halves(keep, send, h, dot(key_dec, head(value_in, h), 0, 0), odd)


def odd_of(mixing):
    return mixing[2:3, 0:HD] > 0.5


def intra_kernel(rows, queries, keys, values, attn, intra):
    for h in range(queries.shape[1] // HD):
        scores = dot(head(queries, h), head(keys, h), 1, 1)
        weights = (scores * mask_of(rows[h:h + 1, :])).astype(BF16)
        attn[h] = weights
        intra[:, lanes_of(h)] = dot(weights, head(values, h), 1, 0)


def scan_kernel(backward, rows, totals, prefix):
    chips, width = totals.shape
    count = width * chips * 2 // HD // HD
    wide = width // count
    row = lax.broadcasted_iota(jnp.int32, (chips, chips), 0)
    col = lax.broadcasted_iota(jnp.int32, (chips, chips), 1)
    far = ((col - row - 1) if backward else (row - col - 1)).astype(F32)
    for h in range(count):
        lanes = slice(h * wide, (h + 1) * wide)
        rate = rows[h:h + 1, 0:chips]
        weight = jnp.where(far >= 0.0, jnp.exp(-(rate * (2.0 * BLOCK)) * jnp.maximum(far, 0.0)), 0.0)
        prefix[:, lanes] = lax.dot_general(
            weight, totals[:, lanes], (((1,), (0,)), ((), ())),
            precision=lax.Precision.HIGHEST, preferred_element_type=F32)


def out_kernel(rows, mixing, queries, out_grad, gain, intra, mine, other, out, held, sums):
    odd = odd_of(mixing)
    square = jnp.zeros((BLOCK, HD), F32)
    cross = jnp.zeros((BLOCK, HD), F32)
    for h in range(queries.shape[1] // HD):
        state = get_state(mine, other, h, odd)
        held[:, lanes_of(h)] = state
        query_dec = scaled(head(queries, h), decay_in_of(short(rows, h)))
        result = head(intra, h) + dot(query_dec, state, 1, 0)
        out[:, lanes_of(h)] = result
        weighted = head(out_grad, h).astype(F32) * head(gain, h)
        square = square + result * result
        cross = cross + weighted * result
    square = jnp.sum(square.T, axis=0, keepdims=True)
    cross = jnp.sum(cross.T, axis=0, keepdims=True)
    both = jnp.concatenate([square, cross], axis=0)
    for peer in range(sums.shape[0]):
        sums[peer] = both


def grad_kernel(rows, mixing, queries, out_grad, gain, out, sums, d_out, keep, send):
    odd = odd_of(mixing)
    total = jnp.sum(sums[...], axis=0)
    inverse = lax.rsqrt(total[0:1] / (HEADS * HD) + epsilon)
    factor = inverse * inverse * inverse * total[1:2] / (HEADS * HD)
    inverse = jnp.broadcast_to(inverse, (HD, BLOCK)).T
    factor = jnp.broadcast_to(factor, (HD, BLOCK)).T
    for h in range(queries.shape[1] // HD):
        weighted = head(out_grad, h).astype(F32) * head(gain, h)
        grad = (weighted * inverse - head(out, h) * factor).astype(BF16)
        d_out[:, lanes_of(h)] = grad
        query_dec = scaled(head(queries, h), decay_in_of(short(rows, h)))
        put_halves(keep, send, h, dot(query_dec, grad, 0, 0), odd)


def local_kernel(rows, queries, keys, values, d_out, held, query_grad, key_part):
    for h in range(queries.shape[1] // HD):
        grad = head(d_out, h)
        back = (dot(grad, head(values, h), 1, 1) * mask_of(rows[h:h + 1, :])).astype(BF16)
        grad_dec = scaled(grad, decay_in_of(short(rows, h)))
        query_grad[:, lanes_of(h)] = (
            dot(back, head(keys, h), 1, 0) + dot(grad_dec, head(held, h), 1, 1)).astype(BF16)
        key_part[:, lanes_of(h)] = dot(back, head(queries, h), 0, 0)


def value_kernel(attn, d_out, value_part):
    for h in range(attn.shape[0]):
        value_part[:, lanes_of(h)] = dot(attn[h], head(d_out, h), 0, 0)


def last_kernel(rows, mixing, keys, values, mine, other, key_part, value_part, key_grad, value_grad):
    odd = odd_of(mixing)
    for h in range(keys.shape[1] // HD):
        later = get_state(mine, other, h, odd)
        decay_out = decay_out_of(short(rows, h))
        value_dec = scaled(head(values, h), decay_out)
        key_dec = scaled(head(keys, h), decay_out)
        key_grad[:, lanes_of(h)] = (head(key_part, h) + dot(value_dec, later, 1, 1)).astype(BF16)
        value_grad[:, lanes_of(h)] = (head(value_part, h) + dot(key_dec, later, 1, 0)).astype(BF16)


def call(body, name, args, shapes, specs=None, scratch=(), flops=0):
    outs = [jax.ShapeDtypeStruct(shape, kind) for shape, kind in shapes]
    moved = sum(a.size * a.dtype.itemsize for a in args)
    return pl.pallas_call(
        body,
        out_shape=outs if len(outs) > 1 else outs[0],
        in_specs=specs or [VMEM] * len(args),
        out_specs=[VMEM] * len(outs) if len(outs) > 1 else VMEM,
        scratch_shapes=list(scratch),
        compiler_params=pltpu.CompilerParams(vmem_limit_bytes=16 * 1024 * 1024),
        cost_estimate=pl.CostEstimate(flops=flops, bytes_accessed=moved, transcendentals=0),
        name=name,
    )(*args)


def scan(keep, send, rows, mixing, beside_first, beside_last, backward):
    chips, width = keep.shape
    partners = [(i, i ^ 1) for i in range(2 * chips)]
    rings = [[2 * i + c for i in range(chips)] for c in range(2)]
    own, coming, add_mine, add_other = (mixing[4 * backward + i][None] for i in range(4))

    got = lax.ppermute(send, "ctx", partners)
    beside_first = beside_first()
    got, beside_first = lax.optimization_barrier((got, beside_first))
    total = own * keep + coming * got
    total = lax.all_to_all(total, "ctx", 0, 0, tiled=True, axis_index_groups=rings)
    prefix = call(functools.partial(scan_kernel, backward), "scan", [rows, total], [((chips, width), F32)])
    prefix = lax.all_to_all(prefix, "ctx", 0, 0, tiled=True, axis_index_groups=rings)
    other = lax.ppermute(own * prefix + add_other * keep, "ctx", partners)
    mine = coming * prefix + add_mine * got
    beside_last = beside_last()
    other, beside_last = lax.optimization_barrier((other, beside_last))
    return mine, other, beside_first, beside_last


def per_device(queries, keys, values, out_grad, rates, gain):
    tokens, width = queries.shape
    count = rates.shape[0]
    chips = lax.axis_size("ctx") // 2
    ranks = lax.axis_size("head")
    half = ((chips, count * HD * HD // 2 // chips), F32)
    gain = gain.reshape(1, width)
    wide16, wide32 = ((BLOCK, width), BF16), ((BLOCK, width), F32)

    keep, send, rows, mixing = call(
        kv_kernel, "kv", [pltpu.with_memory_space_constraint(a, pltpu.HBM) for a in (rates, keys, values)],
        [half, half, ((8, BLOCK), F32), ((8, half[0][1]), F32)],
        specs=[HBM] * 3,
        scratch=[pltpu.SMEM((count,), F32), pltpu.VMEM((BLOCK, width), BF16), pltpu.VMEM((BLOCK, width), BF16),
                 pltpu.SemaphoreType.DMA((2 * count + 1,))])
    mine, other, (attn, intra), unused = scan(
        keep, send, rows, mixing,
        lambda: call(intra_kernel, "intra", [rows, queries, keys, values],
                     [((count, BLOCK, BLOCK), BF16), wide32], flops=4 * BLOCK * BLOCK * width),
        lambda: (), False)
    out, held, sums = call(
        out_kernel, "out", [rows, mixing, queries, out_grad, gain, intra, mine, other],
        [wide32, ((HD, width), BF16), ((ranks, 2, BLOCK), F32)])
    sums = lax.all_to_all(sums, "head", 0, 0, tiled=True)
    d_out, keep, send = call(
        grad_kernel, "grad", [rows, mixing, queries, out_grad, gain, out, sums], [wide16, half, half])
    mine, other, (query_grad, key_part), value_part = scan(
        keep, send, rows, mixing,
        lambda: call(local_kernel, "local", [rows, queries, keys, values, d_out, held], [wide16, wide32],
                     flops=6 * BLOCK * BLOCK * width),
        lambda: call(value_kernel, "value", [attn, d_out], [wide32], flops=2 * BLOCK * BLOCK * width),
        True)
    key_grad, value_grad = call(
        last_kernel, "last", [rows, mixing, keys, values, mine, other, key_part, value_part], [wide16, wide16])
    return query_grad, key_grad, value_grad


def solution(mesh):
    spec = P("ctx", "head")
    return jax.shard_map(
        per_device, mesh=mesh, in_specs=(spec, spec, spec, spec, P("head"), P("head")),
        out_specs=(spec, spec, spec), check_vma=False)
```

```python
import functools

import jax
import jax.numpy as jnp
from jax import lax
from jax.experimental import pallas as pl
from jax.experimental.pallas import tpu as pltpu
from jax.sharding import PartitionSpec as P

HD = 128
HEADS = 40
BLOCK = 256
epsilon = 1e-05

F32 = jnp.float32
BF16 = jnp.bfloat16
VMEM = pl.BlockSpec(memory_space=pltpu.VMEM)
HBM = pl.BlockSpec(memory_space=pltpu.HBM)


def dot(a, b, ca, cb):
    return lax.dot_general(a, b, (((ca,), (cb,)), ((), ())), preferred_element_type=F32)


def lanes_of(h):
    return slice(h * HD, (h + 1) * HD)


def head(ref, h):
    return ref[:, lanes_of(h)]


def decay_in_of(rate):
    place = lax.broadcasted_iota(jnp.int32, (8, HD), 0).astype(F32)
    table = jnp.exp(-rate * (place + 1.0))
    while table.shape[0] < BLOCK:
        step = jnp.exp(jnp.full((1, HD), -float(table.shape[0]), F32) * rate)
        table = jnp.concatenate([table, table * step], axis=0)
    return table


def decay_out_of(rate):
    place = lax.broadcasted_iota(jnp.int32, (8, HD), 0).astype(F32)
    table = jnp.exp(-rate * (7.0 - place))
    while table.shape[0] < BLOCK:
        step = jnp.exp(jnp.full((1, HD), -float(table.shape[0]), F32) * rate)
        table = jnp.concatenate([table * step, table], axis=0)
    return table


def mask_of(rates, decay_in):
    row = lax.broadcasted_iota(jnp.int32, (BLOCK, BLOCK), 0)
    col = lax.broadcasted_iota(jnp.int32, (BLOCK, BLOCK), 1)
    place = lax.broadcasted_iota(jnp.int32, (1, BLOCK), 1).astype(F32)
    growth = jnp.exp(rates * (place + 1.0))
    both = jnp.concatenate([decay_in, decay_in], axis=1) * growth
    return jnp.where(row >= col, both, 0.0)


def short(rows, h):
    return rows[h:h + 1, 0:HD]


def scaled(array, scale):
    return (array.astype(F32) * scale).astype(BF16)


def put_halves(keep, send, h, state, odd):
    chips = keep.shape[0]
    share = HD // 2 // chips
    low, high = state[:HD // 2], state[HD // 2:]
    mine, other = jnp.where(odd, high, low), jnp.where(odd, low, high)
    for r in range(share):
        lane = (h * share + r) * HD
        keep[:, lane:lane + HD] = mine[r * chips:(r + 1) * chips]
        send[:, lane:lane + HD] = other[r * chips:(r + 1) * chips]


def get_half(ref, h):
    chips = ref.shape[0]
    share = HD // 2 // chips
    return jnp.concatenate([ref[:, lanes_of(h * share + r)] for r in range(share)], axis=0)


def get_state(mine, other, h, odd):
    mine, other = get_half(mine, h), get_half(other, h)
    low, high = jnp.where(odd, other, mine), jnp.where(odd, mine, other)
    return jnp.concatenate([low, high], axis=0).astype(BF16)


def kv_kernel(rates, keys, values, keep, send, rows, mixing, rate, key_in, value_in, decays, sems):
    count = rates.shape[0]
    odd = lax.rem(lax.axis_index("ctx"), 2) == 1
    copies = [pltpu.make_async_copy(rates, rate, sems.at[2 * count])]
    for h in range(count):
        for which, (source, target) in enumerate(((keys, key_in), (values, value_in))):
            copies.append(pltpu.make_async_copy(
                source.at[:, lanes_of(h)], target.at[:, lanes_of(h)], sems.at[2 * h + which]))
    for copy in copies:
        copy.start()
    copies[0].wait()
    wide = mixing.shape[1] // count
    index = lax.broadcasted_iota(jnp.int32, (8, wide), 0)
    for h in range(count):
        rows[h:h + 1, :] = jnp.full((1, BLOCK), rate[h], F32)
        decay = jnp.exp(jnp.full((8, wide), -rate[h] * BLOCK, F32))
        place = lax.rem(index, 4)
        later = index >= 4
        first = later == odd
        on_first = jnp.where(place == 0, decay, jnp.where(place == 2, 0.0, 1.0))
        on_second = jnp.where(place == 1, decay, jnp.where(place == 3, 0.0, 1.0))
        mixing[:, h * wide:(h + 1) * wide] = jnp.where(first, on_first, on_second)
        decays[:, lanes_of(h)] = decay_out_of(jnp.full((1, HD), rate[h], F32))
    for h in range(count):
        copies[1 + 2 * h].wait()
        copies[2 + 2 * h].wait()
        key_dec = scaled(head(key_in, h), head(decays, h))
        put_halves(keep, send, h, dot(key_dec, head(value_in, h), 0, 0), odd)


def odd_of(mixing):
    return mixing[2:3, 0:HD] > 0.5


def intra_kernel(rows, queries, keys, values, attn, intra):
    for h in range(queries.shape[1] // HD):
        scores = dot(head(queries, h), head(keys, h), 1, 1)
        weights = (scores * mask_of(rows[h:h + 1, :], decay_in_of(short(rows, h)))).astype(BF16)
        attn[h] = weights
        intra[:, lanes_of(h)] = dot(weights, head(values, h), 1, 0)


def factors(mixing, backward):
    return [mixing[i:i + 1, :] for i in range(4 * backward, 4 * backward + 4)]


def join_kernel(backward, mixing, keep, got, total):
    own, coming = factors(mixing, backward)[:2]
    total[:, 0, :] = own * keep[...] + coming * got[...]


def spread_kernel(backward, mixing, keep, got, prefix, mine, other):
    own, coming, add_mine, add_other = factors(mixing, backward)
    incoming = prefix[:, 0, :]
    other[...] = own * incoming + add_other * keep[...]
    mine[...] = coming * incoming + add_mine * got[...]


def scan_kernel(backward, rows, totals, prefix):
    chips, one, width = totals.shape
    count = width * chips * 2 // HD // HD
    wide = width // count
    row = lax.broadcasted_iota(jnp.int32, (chips, chips), 0)
    col = lax.broadcasted_iota(jnp.int32, (chips, chips), 1)
    far = ((col - row - 1) if backward else (row - col - 1)).astype(F32)
    for h in range(count):
        lanes = slice(h * wide, (h + 1) * wide)
        rate = rows[h:h + 1, 0:chips]
        weight = jnp.where(far >= 0.0, jnp.exp(-(rate * (2.0 * BLOCK)) * jnp.maximum(far, 0.0)), 0.0)
        prefix[:, 0, lanes] = lax.dot_general(
            weight, totals[:, 0, lanes], (((1,), (0,)), ((), ())),
            precision=lax.Precision.HIGHEST, preferred_element_type=F32)


def out_kernel(rows, mixing, queries, out_grad, gain, intra, mine, other, out, held, sums):
    odd = odd_of(mixing)
    square = jnp.zeros((BLOCK, HD), F32)
    cross = jnp.zeros((BLOCK, HD), F32)
    for h in range(queries.shape[1] // HD):
        state = get_state(mine, other, h, odd)
        held[:, lanes_of(h)] = state
        query_dec = scaled(head(queries, h), decay_in_of(short(rows, h)))
        result = head(intra, h) + dot(query_dec, state, 1, 0)
        out[:, lanes_of(h)] = result
        weighted = head(out_grad, h).astype(F32) * head(gain, h)
        square = square + result * result
        cross = cross + weighted * result
    square = jnp.sum(square.T, axis=0, keepdims=True)
    cross = jnp.sum(cross.T, axis=0, keepdims=True)
    both = jnp.concatenate([square, cross], axis=0)
    for peer in range(sums.shape[0]):
        sums[peer] = both


def grad_kernel(rows, mixing, queries, out_grad, gain, out, sums, d_out, keep, send):
    odd = odd_of(mixing)
    total = jnp.sum(sums[...], axis=0)
    inverse = lax.rsqrt(total[0:1] / (HEADS * HD) + epsilon)
    factor = inverse * inverse * inverse * total[1:2] / (HEADS * HD)
    inverse = jnp.broadcast_to(inverse, (HD, BLOCK)).T
    factor = jnp.broadcast_to(factor, (HD, BLOCK)).T
    for h in range(queries.shape[1] // HD):
        weighted = head(out_grad, h).astype(F32) * head(gain, h)
        grad = (weighted * inverse - head(out, h) * factor).astype(BF16)
        d_out[:, lanes_of(h)] = grad
        query_dec = scaled(head(queries, h), decay_in_of(short(rows, h)))
        put_halves(keep, send, h, dot(query_dec, grad, 0, 0), odd)


def local_kernel(rows, keys, values, d_out, held, query_grad, back_attn):
    for h in range(keys.shape[1] // HD):
        grad = head(d_out, h)
        decay_in = decay_in_of(short(rows, h))
        back = (dot(grad, head(values, h), 1, 1) * mask_of(rows[h:h + 1, :], decay_in)).astype(BF16)
        back_attn[h] = back
        query_grad[:, lanes_of(h)] = (
            dot(back, head(keys, h), 1, 0) + dot(scaled(grad, decay_in), head(held, h), 1, 1)).astype(BF16)


def parts_kernel(queries, attn, back_attn, d_out, key_part, value_part):
    for h in range(attn.shape[0]):
        key_part[:, lanes_of(h)] = dot(back_attn[h], head(queries, h), 0, 0)
        value_part[:, lanes_of(h)] = dot(attn[h], head(d_out, h), 0, 0)


def last_kernel(rows, mixing, keys, values, mine, other, key_part, value_part,
                key_grad, value_grad, key_out, value_out, sems):
    odd = odd_of(mixing)
    copies = []
    for h in range(keys.shape[1] // HD):
        later = get_state(mine, other, h, odd)
        decay_out = decay_out_of(short(rows, h))
        value_dec = scaled(head(values, h), decay_out)
        key_dec = scaled(head(keys, h), decay_out)
        key_out[:, lanes_of(h)] = (head(key_part, h) + dot(value_dec, later, 1, 1)).astype(BF16)
        value_out[:, lanes_of(h)] = (head(value_part, h) + dot(key_dec, later, 1, 0)).astype(BF16)
        for which, (source, target) in enumerate(((key_out, key_grad), (value_out, value_grad))):
            copies.append(pltpu.make_async_copy(
                source.at[:, lanes_of(h)], target.at[:, lanes_of(h)], sems.at[2 * h + which]))
            copies[-1].start()
    for copy in copies:
        copy.wait()


def call(body, name, args, shapes, specs=None, scratch=(), flops=0, into=VMEM):
    outs = [jax.ShapeDtypeStruct(shape, kind) for shape, kind in shapes]
    moved = sum(a.size * a.dtype.itemsize for a in args)
    return pl.pallas_call(
        body,
        out_shape=outs if len(outs) > 1 else outs[0],
        in_specs=specs or [VMEM] * len(args),
        out_specs=[into] * len(outs) if len(outs) > 1 else into,
        scratch_shapes=list(scratch),
        compiler_params=pltpu.CompilerParams(vmem_limit_bytes=16 * 1024 * 1024),
        cost_estimate=pl.CostEstimate(flops=flops, bytes_accessed=moved, transcendentals=0),
        name=name,
    )(*args)


def scan(keep, send, rows, mixing, beside_first, beside_last, backward):
    chips, width = keep.shape
    partners = [(i, i ^ 1) for i in range(2 * chips)]
    rings = [[2 * i + c for i in range(chips)] for c in range(2)]
    flat = ((chips, 1, width), F32)

    got = lax.ppermute(send, "ctx", partners)
    first = beside_first()
    got, first = lax.optimization_barrier((got, first))
    total = call(functools.partial(join_kernel, backward), "join", [mixing, keep, got], [flat])
    total = lax.all_to_all(total, "ctx", 0, 0, tiled=True, axis_index_groups=rings)
    prefix = call(functools.partial(scan_kernel, backward), "scan", [rows, total], [flat])
    prefix = lax.all_to_all(prefix, "ctx", 0, 0, tiled=True, axis_index_groups=rings)
    mine, other = call(
        functools.partial(spread_kernel, backward), "spread", [mixing, keep, got, prefix],
        [((chips, width), F32)] * 2)
    other = lax.ppermute(other, "ctx", partners)
    last = beside_last(first)
    other, last = lax.optimization_barrier((other, last))
    return mine, other, first, last


def per_device(queries, keys, values, out_grad, rates, gain):
    tokens, width = queries.shape
    count = rates.shape[0]
    chips = lax.axis_size("ctx") // 2
    ranks = lax.axis_size("head")
    half = ((chips, count * HD * HD // 2 // chips), F32)
    gain = gain.reshape(1, width)
    wide16, wide32 = ((BLOCK, width), BF16), ((BLOCK, width), F32)

    keep, send, rows, mixing = call(
        kv_kernel, "kv", [pltpu.with_memory_space_constraint(a, pltpu.HBM) for a in (rates, keys, values)],
        [half, half, ((8, BLOCK), F32), ((8, half[0][1]), F32)],
        specs=[HBM] * 3,
        scratch=[pltpu.SMEM((count,), F32), pltpu.VMEM((BLOCK, width), BF16), pltpu.VMEM((BLOCK, width), BF16),
                 pltpu.VMEM((BLOCK, width), F32),
                 pltpu.SemaphoreType.DMA((2 * count + 1,))])
    mine, other, unused, (attn, intra) = scan(
        keep, send, rows, mixing, lambda: (),
        lambda first: call(intra_kernel, "intra", [rows, queries, keys, values],
                           [((count, BLOCK, BLOCK), BF16), wide32], flops=4 * BLOCK * BLOCK * width),
        False)
    out, held, sums = call(
        out_kernel, "out", [rows, mixing, queries, out_grad, gain, intra, mine, other],
        [wide32, ((HD, width), BF16), ((ranks, 2, BLOCK), F32)])
    sums = lax.all_to_all(sums, "head", 0, 0, tiled=True)
    d_out, keep, send = call(
        grad_kernel, "grad", [rows, mixing, queries, out_grad, gain, out, sums], [wide16, half, half])
    mine, other, (query_grad, unused), (key_part, value_part) = scan(
        keep, send, rows, mixing,
        lambda: call(local_kernel, "local", [rows, keys, values, d_out, held],
                     [wide16, ((count, BLOCK, BLOCK), BF16)], flops=4 * BLOCK * BLOCK * width),
        lambda first: call(parts_kernel, "parts", [queries, attn, first[1], d_out], [wide32, wide32],
                           flops=4 * BLOCK * BLOCK * width),
        True)
    key_grad, value_grad = call(
        last_kernel, "last", [rows, mixing, keys, values, mine, other, key_part, value_part], [wide16, wide16],
        scratch=[pltpu.VMEM((BLOCK, width), BF16), pltpu.VMEM((BLOCK, width), BF16),
                 pltpu.SemaphoreType.DMA((2 * count,))],
        into=HBM)
    return query_grad, key_grad, value_grad


def solution(mesh):
    spec = P("ctx", "head")
    return jax.shard_map(
        per_device, mesh=mesh, in_specs=(spec, spec, spec, spec, P("head"), P("head")),
        out_specs=(spec, spec, spec), check_vma=False)
```

```python
import functools

import jax
import jax.numpy as jnp
from jax import lax
from jax.experimental import pallas as pl
from jax.experimental.pallas import tpu as pltpu
from jax.sharding import PartitionSpec as P

HD = 128
HEADS = 40
BLOCK = 256
epsilon = 1e-05

HALF = HD // 2
F32 = jnp.float32
BF16 = jnp.bfloat16
VMEM = pl.BlockSpec(memory_space=pltpu.VMEM)
HBM = pl.BlockSpec(memory_space=pltpu.HBM)


def dot(a, b, ca, cb):
    return lax.dot_general(a, b, (((ca,), (cb,)), ((), ())), preferred_element_type=F32)


def lanes_of(h):
    return slice(h * HD, (h + 1) * HD)


def head(ref, h):
    return ref[:, lanes_of(h)]


def decay_in_of(rate):
    place = lax.broadcasted_iota(jnp.int32, (8, HD), 0).astype(F32)
    table = jnp.exp(-rate * (place + 1.0))
    while table.shape[0] < BLOCK:
        step = jnp.exp(jnp.full((1, HD), -float(table.shape[0]), F32) * rate)
        table = jnp.concatenate([table, table * step], axis=0)
    return table


def decay_out_of(rate):
    place = lax.broadcasted_iota(jnp.int32, (8, HD), 0).astype(F32)
    table = jnp.exp(-rate * (7.0 - place))
    while table.shape[0] < BLOCK:
        step = jnp.exp(jnp.full((1, HD), -float(table.shape[0]), F32) * rate)
        table = jnp.concatenate([table * step, table], axis=0)
    return table


def mask_of(rates, decay_in):
    row = lax.broadcasted_iota(jnp.int32, (BLOCK, BLOCK), 0)
    col = lax.broadcasted_iota(jnp.int32, (BLOCK, BLOCK), 1)
    place = lax.broadcasted_iota(jnp.int32, (1, BLOCK), 1).astype(F32)
    growth = jnp.exp(rates * (place + 1.0))
    both = jnp.concatenate([decay_in, decay_in], axis=1) * growth
    return jnp.where(row >= col, both, 0.0)


def short(rows, h):
    return rows[h:h + 1, 0:HD]


def scaled(array, scale):
    return (array.astype(F32) * scale).astype(BF16)


def put_halves(keep, send, h, state, odd):
    chips = keep.shape[0]
    share = HD // 2 // chips
    low, high = state[:HD // 2], state[HD // 2:]
    mine, other = jnp.where(odd, high, low), jnp.where(odd, low, high)
    for r in range(share):
        lane = (h * share + r) * HD
        keep[:, lane:lane + HD] = mine[r * chips:(r + 1) * chips]
        send[:, lane:lane + HD] = other[r * chips:(r + 1) * chips]


def put_half(ref, h, state):
    chips = ref.shape[0]
    share = HD // 2 // chips
    for r in range(share):
        lane = (h * share + r) * HD
        ref[:, lane:lane + HD] = state[r * chips:(r + 1) * chips]


def get_half(ref, h):
    chips = ref.shape[0]
    share = HD // 2 // chips
    return jnp.concatenate([ref[:, lanes_of(h * share + r)] for r in range(share)], axis=0)


def rows_of(h, size, start=0):
    return slice(start + h * size, start + (h + 1) * size)


def whole(mine, other, odd):
    low, high = jnp.where(odd, other, mine), jnp.where(odd, mine, other)
    return jnp.concatenate([low, high], axis=0)


def get_state(mine, other, h, odd):
    return whole(get_half(mine, h), get_half(other, h), odd).astype(BF16)


def kv_kernel(rates, keys, values, queries, out_grad, keep, send, rows, mixing, key_in, value_in, query_in, grad_in,
              rate, decays, sems):
    count = rates.shape[0]
    odd = lax.rem(lax.axis_index("ctx"), 2) == 1
    copies = [pltpu.make_async_copy(rates, rate, sems.at[0])]
    for h in range(count):
        for source, target in ((keys, key_in), (values, value_in)):
            copies.append(pltpu.make_async_copy(
                source.at[:, lanes_of(h)], target.at[:, lanes_of(h)], sems.at[len(copies)]))
    for source, target in ((queries, query_in), (out_grad, grad_in)):
        copies.append(pltpu.make_async_copy(source, target, sems.at[len(copies)]))
    for copy in copies:
        copy.start()
    copies[0].wait()
    wide = mixing.shape[1] // count
    index = lax.broadcasted_iota(jnp.int32, (8, wide), 0)
    for h in range(count):
        rows[h:h + 1, :] = jnp.full((1, BLOCK), rate[h], F32)
        decay = jnp.exp(jnp.full((8, wide), -rate[h] * BLOCK, F32))
        place = lax.rem(index, 4)
        later = index >= 4
        first = later == odd
        on_first = jnp.where(place == 0, decay, jnp.where(place == 2, 0.0, 1.0))
        on_second = jnp.where(place == 1, decay, jnp.where(place == 3, 0.0, 1.0))
        mixing[:, h * wide:(h + 1) * wide] = jnp.where(first, on_first, on_second)
        decays[:, lanes_of(h)] = decay_out_of(jnp.full((1, HD), rate[h], F32))
    for h in range(count):
        copies[1 + 2 * h].wait()
        copies[2 + 2 * h].wait()
        key_dec = scaled(head(key_in, h), head(decays, h))
        put_halves(keep, send, h, dot(head(value_in, h), key_dec, 0, 0), odd)
    for copy in copies[1 + 2 * count:]:
        copy.wait()


def odd_of(mixing, width=HD):
    return mixing[2:3, 0:width] > 0.5


def intra_kernel(rows, mixing, queries, keys, values, out_grad, gain, attn, query_t, intra_t, weighted_t, partner):
    odd = odd_of(mixing, BLOCK)
    count = queries.shape[1] // HD
    for h in range(count):
        decay_in = decay_in_of(short(rows, h))
        scores = dot(head(queries, h), head(keys, h), 1, 1)
        weights = (scores * mask_of(rows[h:h + 1, :], decay_in)).astype(BF16)
        attn[h] = weights
        query_dec = scaled(head(queries, h), decay_in).astype(F32).T
        query_t[rows_of(h, HD), :] = query_dec.astype(BF16)
        partner[rows_of(h, HD), :] = query_dec
        intra = dot(head(values, h), weights, 0, 1)
        weighted = (head(out_grad, h).astype(F32) * head(gain, h)).T
        start = count * HD
        for array, target in ((intra, intra_t), (weighted, weighted_t)):
            low, high = array[:HALF], array[HALF:]
            target[rows_of(h, HALF), :] = jnp.where(odd, high, low)
            partner[rows_of(h, HALF, start), :] = jnp.where(odd, low, high)
            start += count * HALF


def factors(mixing, backward):
    return [mixing[i:i + 1, :] for i in range(4 * backward, 4 * backward + 4)]


def join_kernel(backward, mixing, keep, got, total):
    own, coming = factors(mixing, backward)[:2]
    total[:, 0, :] = own * keep[...] + coming * got[...]


def spread_kernel(backward, mixing, base, prefix, mine, other):
    own, coming, add_mine, add_other = factors(mixing, backward)
    incoming = prefix[:, 0, :]
    other[...] = own * incoming + add_other * base[...]
    mine[...] = coming * incoming + add_mine * base[...]


def scan_kernel(backward, rows, totals, prefix):
    chips, one, width = totals.shape
    count = width * chips * 2 // HD // HD
    wide = width // count
    row = lax.broadcasted_iota(jnp.int32, (chips, chips), 0)
    col = lax.broadcasted_iota(jnp.int32, (chips, chips), 1)
    far = ((col - row - 1) if backward else (row - col - 1)).astype(F32)
    for h in range(count):
        lanes = slice(h * wide, (h + 1) * wide)
        rate = rows[h:h + 1, 0:chips]
        weight = jnp.where(far >= 0.0, jnp.exp(-(rate * (2.0 * BLOCK)) * jnp.maximum(far, 0.0)), 0.0)
        prefix[:, 0, lanes] = lax.dot_general(
            weight, totals[:, 0, lanes], (((1,), (0,)), ((), ())),
            precision=lax.Precision.HIGHEST, preferred_element_type=F32)


def fold(array):
    return jnp.sum(array.reshape(HALF // 8, 8, BLOCK), axis=0)


def blocks_of(h, count, query_t, intra_t, weighted_t, partner):
    mine = (query_t[rows_of(h, HD), :], intra_t[rows_of(h, HALF), :], weighted_t[rows_of(h, HALF), :])
    other = (partner[rows_of(h, HD), :].astype(BF16), partner[rows_of(h, HALF, count * HD), :],
             partner[rows_of(h, HALF, count * (HD + HALF)), :])
    return mine, other


def out_kernel(mixing, keep, got, prefix, query_t, intra_t, weighted_t, partner, out, held, sums):
    chips, width = keep.shape
    count = query_t.shape[0] // HD
    wide = width // count
    share = wide // HD
    sums_of = [[jnp.zeros((8, BLOCK), F32) for _ in range(2)] for _ in range(2)]
    for h in range(count):
        own, coming, add_mine, add_other = (row[:, h * wide:h * wide + HD] for row in factors(mixing, False))
        incoming = jnp.concatenate([prefix[:, 0, lanes_of(h * share + r)] for r in range(share)], axis=0)
        states = (coming * incoming + add_mine * get_half(got, h), own * incoming + add_other * get_half(keep, h))
        for which, (query, intra, weighted) in enumerate(blocks_of(h, count, query_t, intra_t, weighted_t, partner)):
            state = states[which].astype(BF16)
            held[which, rows_of(h, HALF), :] = state.astype(F32)
            result = intra + dot(state, query, 1, 0)
            out[which, rows_of(h, HALF), :] = result
            sums_of[which][0] = sums_of[which][0] + fold(result * result)
            sums_of[which][1] = sums_of[which][1] + fold(weighted * result)
    odd = odd_of(mixing, BLOCK)
    mine, other = ([jnp.sum(part, axis=0, keepdims=True) for part in parts] for parts in sums_of)
    even_block = [jnp.where(odd, b, a) for a, b in zip(mine, other)]
    odd_block = [jnp.where(odd, a, b) for a, b in zip(mine, other)]
    both = jnp.concatenate(even_block + odd_block, axis=0)
    for peer in range(sums.shape[0]):
        sums[peer] = both


def pack_kernel(grad_t, held, exchange):
    exchange[:, 0:BLOCK] = grad_t[1].astype(F32)
    exchange[:, BLOCK:BLOCK + HD] = held[1]


def grad_kernel(mixing, sums, out, query_t, intra_t, weighted_t, partner, total, base, grad_t):
    odd = odd_of(mixing, BLOCK)
    count = query_t.shape[0] // HD
    first = mixing[7:8, 0:HD] > 0.5
    chips, one, width = total.shape
    wide = width // count
    share = wide // HD
    summed = jnp.sum(sums[...], axis=0)
    even_block, odd_block = summed[0:2], summed[2:4]
    scales = []
    for block in (jnp.where(odd, odd_block, even_block), jnp.where(odd, even_block, odd_block)):
        inverse = lax.rsqrt(block[0:1] / (HEADS * HD) + epsilon)
        scales.append((inverse, inverse * inverse * inverse * block[1:2] / (HEADS * HD)))
    for h in range(count):
        own, coming = (row[:, h * wide:h * wide + HD] for row in factors(mixing, True)[:2])
        terms = []
        for which, (query, intra, weighted) in enumerate(blocks_of(h, count, query_t, intra_t, weighted_t, partner)):
            inverse, factor = scales[which]
            grad = (weighted * inverse - out[which, rows_of(h, HALF), :] * factor).astype(BF16)
            grad_t[which, rows_of(h, HALF), :] = grad
            terms.append(dot(grad, query, 1, 1))
        put_half(base, h, jnp.where(first, terms[0], terms[1]))
        joined = own * terms[0] + coming * terms[1]
        for r in range(share):
            total[:, 0, lanes_of(h * share + r)] = joined[r * chips:(r + 1) * chips]


def local_kernel(rows, mixing, keys, values, grad_t, held, exchange, query_grad, back_attn, whole_grad):
    for h in range(keys.shape[1] // HD):
        place = lax.broadcasted_iota(jnp.int32, (1, BLOCK), 1).astype(F32)
        grad = whole(grad_t[0, rows_of(h, HALF), :].astype(F32), exchange[rows_of(h, HALF), 0:BLOCK], odd_of(mixing, BLOCK))
        state = whole(held[0, rows_of(h, HALF), :], exchange[rows_of(h, HALF), BLOCK:BLOCK + HD], odd_of(mixing))
        grad_dec = (grad * jnp.exp(-rows[h:h + 1, :] * (place + 1.0))).astype(BF16)
        grad = grad.astype(BF16)
        whole_grad[rows_of(h, HD), :] = grad
        mask = mask_of(rows[h:h + 1, :], decay_in_of(short(rows, h)))
        back = (dot(grad, head(values, h), 0, 1) * mask).astype(BF16)
        back_attn[h] = back
        query_grad[:, lanes_of(h)] = (
            dot(back, head(keys, h), 1, 0) + dot(grad_dec, state.astype(BF16), 0, 0)).astype(BF16)


def parts_kernel(queries, attn, back_attn, whole_grad, key_part, value_part):
    for h in range(attn.shape[0]):
        key_part[:, lanes_of(h)] = dot(back_attn[h], head(queries, h), 0, 0)
        value_part[:, lanes_of(h)] = dot(attn[h], whole_grad[rows_of(h, HD), :], 0, 1)


def last_kernel(rows, mixing, keys, values, mine, other, key_part, value_part,
                key_grad, value_grad, key_out, value_out, sems):
    odd = odd_of(mixing)
    copies = []
    for h in range(keys.shape[1] // HD):
        later = get_state(mine, other, h, odd)
        decay_out = decay_out_of(short(rows, h))
        value_dec = scaled(head(values, h), decay_out)
        key_dec = scaled(head(keys, h), decay_out)
        key_out[:, lanes_of(h)] = (head(key_part, h) + dot(value_dec, later, 1, 0)).astype(BF16)
        value_out[:, lanes_of(h)] = (head(value_part, h) + dot(key_dec, later, 1, 1)).astype(BF16)
        for which, (source, target) in enumerate(((key_out, key_grad), (value_out, value_grad))):
            copies.append(pltpu.make_async_copy(
                source.at[:, lanes_of(h)], target.at[:, lanes_of(h)], sems.at[2 * h + which]))
            copies[-1].start()
    for copy in copies:
        copy.wait()


def call(body, name, args, shapes, specs=None, scratch=(), flops=0, into=VMEM):
    outs = [jax.ShapeDtypeStruct(shape, kind) for shape, kind in shapes]
    moved = sum(a.size * a.dtype.itemsize for a in args)
    return pl.pallas_call(
        body,
        out_shape=outs if len(outs) > 1 else outs[0],
        in_specs=specs or [VMEM] * len(args),
        out_specs=[into] * len(outs) if len(outs) > 1 else into,
        scratch_shapes=list(scratch),
        compiler_params=pltpu.CompilerParams(vmem_limit_bytes=16 * 1024 * 1024),
        cost_estimate=pl.CostEstimate(flops=flops, bytes_accessed=moved, transcendentals=0),
        name=name,
    )(*args)


def per_device(queries, keys, values, out_grad, rates, gain):
    tokens, width = queries.shape
    count = rates.shape[0]
    chips = lax.axis_size("ctx") // 2
    ranks = lax.axis_size("head")
    lanes = count * HD * HALF // chips
    half, flat, rows_half = ((chips, lanes), F32), ((chips, 1, lanes), F32), ((count * HALF, BLOCK), F32)
    gain = gain.reshape(1, width)
    wide16, wide32 = ((BLOCK, width), BF16), ((BLOCK, width), F32)
    square = ((count, BLOCK, BLOCK), BF16)
    unit = BLOCK * BLOCK * width
    partners = [(i, i ^ 1) for i in range(2 * chips)]
    rings = [[2 * i + c for i in range(chips)] for c in range(2)]
    towers = [[(2 * i + c) * ranks + y for c in range(2) for y in range(ranks)] for i in range(chips)]

    def swap(array):
        return lax.ppermute(array, "ctx", partners)

    def spread_out(array):
        return lax.all_to_all(array, "ctx", 0, 0, tiled=True, axis_index_groups=rings)

    keep, send, rows, mixing, key_in, value_in, query_in, grad_in = call(
        kv_kernel, "kv", [pltpu.with_memory_space_constraint(a, pltpu.HBM) for a in (rates, keys, values, queries, out_grad)],
        [half, half, ((8, BLOCK), F32), ((8, lanes), F32)] + [wide16] * 4,
        specs=[HBM] * 5,
        scratch=[pltpu.SMEM((count,), F32), pltpu.VMEM((BLOCK, width), F32),
                 pltpu.SemaphoreType.DMA((2 * count + 3,))])
    got = swap(send)
    attn, query_t, intra_t, weighted_t, partner = call(
        intra_kernel, "intra", [rows, mixing, query_in, key_in, value_in, grad_in, gain],
        [square, ((width, BLOCK), BF16), rows_half, rows_half, ((2 * width, BLOCK), F32)], flops=4 * unit)
    got, partner = lax.optimization_barrier((got, partner))
    total = call(functools.partial(join_kernel, False), "join", [mixing, keep, got], [flat])
    total = spread_out(total)
    prefix = call(functools.partial(scan_kernel, False), "scan", [rows, total], [flat])
    prefix, partner = lax.optimization_barrier((prefix, partner))
    partner = swap(partner)
    prefix = spread_out(prefix)
    shared = [query_t, intra_t, weighted_t, partner]
    out, held, sums = call(
        out_kernel, "out", [mixing, keep, got, prefix] + shared,
        [((2, count * HALF, BLOCK), F32), ((2, count * HALF, HD), F32), ((2 * ranks, 4, BLOCK), F32)])
    sums = lax.all_to_all(sums, ("ctx", "head"), 0, 0, tiled=True, axis_index_groups=towers)
    total, base, grad_t = call(
        grad_kernel, "grad", [mixing, sums, out] + shared,
        [flat, half, ((2, count * HALF, BLOCK), BF16)])
    total = spread_out(total)
    exchange = swap(call(pack_kernel, "pack", [grad_t, held], [((count * HALF, BLOCK + HD), F32)], flops=4 * unit))
    prefix = spread_out(call(functools.partial(scan_kernel, True), "scan", [rows, total], [flat]))
    mine, other = call(
        functools.partial(spread_kernel, True), "spread", [mixing, base, prefix], [half, half])
    tied, other = lax.optimization_barrier((rows, other))
    other = swap(other)
    query_grad, back_attn, whole_grad = call(
        local_kernel, "local", [tied, mixing, keys, values, grad_t, held, exchange],
        [wide16, square, ((width, BLOCK), BF16)], flops=4 * unit)
    key_part, value_part = call(
        parts_kernel, "parts", [queries, attn, back_attn, whole_grad], [wide32, wide32], flops=4 * unit)
    other, key_part, value_part = lax.optimization_barrier((other, key_part, value_part))
    key_grad, value_grad = call(
        last_kernel, "last", [rows, mixing, keys, values, mine, other, key_part, value_part], [wide16, wide16],
        scratch=[pltpu.VMEM((BLOCK, width), BF16), pltpu.VMEM((BLOCK, width), BF16),
                 pltpu.SemaphoreType.DMA((2 * count,))],
        into=HBM)
    return query_grad, key_grad, value_grad


def solution(mesh):
    spec = P("ctx", "head")
    return jax.shard_map(
        per_device, mesh=mesh, in_specs=(spec, spec, spec, spec, P("head"), P("head")),
        out_specs=(spec, spec, spec), check_vma=False)
```

```python
import functools

import jax
import jax.numpy as jnp
from jax import lax
from jax.experimental import pallas as pl
from jax.experimental.pallas import tpu as pltpu
from jax.sharding import PartitionSpec as P

HD = 128
HEADS = 40
BLOCK = 256
epsilon = 1e-05

HALF = HD // 2
F32 = jnp.float32
BF16 = jnp.bfloat16
VMEM = pl.BlockSpec(memory_space=pltpu.VMEM)
HBM = pl.BlockSpec(memory_space=pltpu.HBM)


def dot(a, b, ca, cb):
    return lax.dot_general(a, b, (((ca,), (cb,)), ((), ())), preferred_element_type=F32)


def lanes_of(h):
    return slice(h * HD, (h + 1) * HD)


def head(ref, h):
    return ref[:, lanes_of(h)]


def decay_in_of(rate):
    place = lax.broadcasted_iota(jnp.int32, (8, HD), 0).astype(F32)
    table = jnp.exp(-rate * (place + 1.0))
    while table.shape[0] < BLOCK:
        step = jnp.exp(jnp.full((1, HD), -float(table.shape[0]), F32) * rate)
        table = jnp.concatenate([table, table * step], axis=0)
    return table


def decay_out_of(rate):
    place = lax.broadcasted_iota(jnp.int32, (8, HD), 0).astype(F32)
    table = jnp.exp(-rate * (7.0 - place))
    while table.shape[0] < BLOCK:
        step = jnp.exp(jnp.full((1, HD), -float(table.shape[0]), F32) * rate)
        table = jnp.concatenate([table * step, table], axis=0)
    return table


def mask_of(rates, decay_in):
    row = lax.broadcasted_iota(jnp.int32, (BLOCK, BLOCK), 0)
    col = lax.broadcasted_iota(jnp.int32, (BLOCK, BLOCK), 1)
    place = lax.broadcasted_iota(jnp.int32, (1, BLOCK), 1).astype(F32)
    growth = jnp.exp(rates * (place + 1.0))
    both = jnp.concatenate([decay_in, decay_in], axis=1) * growth
    return jnp.where(row >= col, both, 0.0)


def short(rows, h):
    return rows[h:h + 1, 0:HD]


def scaled(array, scale):
    return (array.astype(F32) * scale).astype(BF16)


def put_halves(keep, send, h, state, odd):
    chips = keep.shape[0]
    share = HD // 2 // chips
    low, high = state[:HD // 2], state[HD // 2:]
    mine, other = jnp.where(odd, high, low), jnp.where(odd, low, high)
    for r in range(share):
        lane = (h * share + r) * HD
        keep[:, lane:lane + HD] = mine[r * chips:(r + 1) * chips]
        send[:, lane:lane + HD] = other[r * chips:(r + 1) * chips]


def put_half(ref, h, state):
    chips = ref.shape[0]
    share = HD // 2 // chips
    for r in range(share):
        lane = (h * share + r) * HD
        ref[:, lane:lane + HD] = state[r * chips:(r + 1) * chips]


def get_half(ref, h):
    chips = ref.shape[0]
    share = HD // 2 // chips
    return jnp.concatenate([ref[:, lanes_of(h * share + r)] for r in range(share)], axis=0)


def rows_of(h, size, start=0):
    return slice(start + h * size, start + (h + 1) * size)


def whole(mine, other, odd):
    low, high = jnp.where(odd, other, mine), jnp.where(odd, mine, other)
    return jnp.concatenate([low, high], axis=0)


def get_state(mine, other, h, odd):
    return whole(get_half(mine, h), get_half(other, h), odd).astype(BF16)


def kv_kernel(rates, keys, values, queries, out_grad, keep, send, rows, mixing, key_in, value_in, query_in, grad_in,
              rate, decays, sems):
    count = rates.shape[0]
    odd = lax.rem(lax.axis_index("ctx"), 2) == 1
    pairs = ((rates, rate), (keys, key_in), (values, value_in), (queries, query_in), (out_grad, grad_in))
    copies = [pltpu.make_async_copy(source, target, sems.at[i]) for i, (source, target) in enumerate(pairs)]
    for copy in copies:
        copy.start()
    copies[0].wait()
    wide = mixing.shape[1] // count
    index = lax.broadcasted_iota(jnp.int32, (8, wide), 0)
    for h in range(count):
        rows[h:h + 1, :] = jnp.full((1, BLOCK), rate[h], F32)
        decay = jnp.exp(jnp.full((8, wide), -rate[h] * BLOCK, F32))
        place = lax.rem(index, 4)
        later = index >= 4
        first = later == odd
        on_first = jnp.where(place == 0, decay, jnp.where(place == 2, 0.0, 1.0))
        on_second = jnp.where(place == 1, decay, jnp.where(place == 3, 0.0, 1.0))
        mixing[:, h * wide:(h + 1) * wide] = jnp.where(first, on_first, on_second)
        decays[:, lanes_of(h)] = decay_out_of(jnp.full((1, HD), rate[h], F32))
    copies[1].wait()
    copies[2].wait()
    for h in range(count):
        key_dec = scaled(head(key_in, h), head(decays, h))
        put_halves(keep, send, h, dot(head(value_in, h), key_dec, 0, 0), odd)
    copies[3].wait()
    copies[4].wait()


def odd_of(mixing, width=HD):
    return mixing[2:3, 0:width] > 0.5


def intra_kernel(rows, mixing, queries, keys, values, out_grad, gain, attn, query_t, intra_t, weighted_t, partner):
    odd = odd_of(mixing, BLOCK)
    count = queries.shape[1] // HD
    for h in range(count):
        decay_in = decay_in_of(short(rows, h))
        scores = dot(head(queries, h), head(keys, h), 1, 1)
        weights = (scores * mask_of(rows[h:h + 1, :], decay_in)).astype(BF16)
        attn[h] = weights
        query_dec = scaled(head(queries, h), decay_in).astype(F32).T
        query_t[rows_of(h, HD), :] = query_dec.astype(BF16)
        partner[rows_of(h, HD), :] = query_dec
        intra = dot(head(values, h), weights, 0, 1)
        weighted = (head(out_grad, h).astype(F32) * head(gain, h)).T
        start = count * HD
        for array, target in ((intra, intra_t), (weighted, weighted_t)):
            low, high = array[:HALF], array[HALF:]
            target[rows_of(h, HALF), :] = jnp.where(odd, high, low)
            partner[rows_of(h, HALF, start), :] = jnp.where(odd, low, high)
            start += count * HALF


def factors(mixing, backward):
    return [mixing[i:i + 1, :] for i in range(4 * backward, 4 * backward + 4)]


def join_kernel(backward, mixing, keep, got, total):
    own, coming = factors(mixing, backward)[:2]
    total[:, 0, :] = own * keep[...] + coming * got[...]


def spread_kernel(backward, mixing, base, prefix, mine, other):
    own, coming, add_mine, add_other = factors(mixing, backward)
    incoming = prefix[:, 0, :]
    other[...] = own * incoming + add_other * base[...]
    mine[...] = coming * incoming + add_mine * base[...]


def scan_kernel(backward, rows, totals, prefix):
    chips, one, width = totals.shape
    count = width * chips * 2 // HD // HD
    wide = width // count
    row = lax.broadcasted_iota(jnp.int32, (chips, chips), 0)
    col = lax.broadcasted_iota(jnp.int32, (chips, chips), 1)
    far = ((col - row - 1) if backward else (row - col - 1)).astype(F32)
    for h in range(count):
        lanes = slice(h * wide, (h + 1) * wide)
        rate = rows[h:h + 1, 0:chips]
        weight = jnp.where(far >= 0.0, jnp.exp(-(rate * (2.0 * BLOCK)) * jnp.maximum(far, 0.0)), 0.0)
        prefix[:, 0, lanes] = lax.dot_general(
            weight, totals[:, 0, lanes], (((1,), (0,)), ((), ())),
            precision=lax.Precision.HIGHEST, preferred_element_type=F32)


def fold(array):
    return jnp.sum(array.reshape(HALF // 8, 8, BLOCK), axis=0)


def blocks_of(h, count, query_t, intra_t, weighted_t, partner):
    mine = (query_t[rows_of(h, HD), :], intra_t[rows_of(h, HALF), :], weighted_t[rows_of(h, HALF), :])
    other = (partner[rows_of(h, HD), :].astype(BF16), partner[rows_of(h, HALF, count * HD), :],
             partner[rows_of(h, HALF, count * (HD + HALF)), :])
    return mine, other


def out_kernel(mixing, keep, got, prefix, query_t, intra_t, weighted_t, partner, out, held, sums):
    chips, width = keep.shape
    count = query_t.shape[0] // HD
    wide = width // count
    share = wide // HD
    sums_of = [[jnp.zeros((8, BLOCK), F32) for _ in range(2)] for _ in range(2)]
    for h in range(count):
        own, coming, add_mine, add_other = (row[:, h * wide:h * wide + HD] for row in factors(mixing, False))
        incoming = jnp.concatenate([prefix[:, 0, lanes_of(h * share + r)] for r in range(share)], axis=0)
        states = (coming * incoming + add_mine * get_half(got, h), own * incoming + add_other * get_half(keep, h))
        for which, (query, intra, weighted) in enumerate(blocks_of(h, count, query_t, intra_t, weighted_t, partner)):
            state = states[which].astype(BF16)
            held[which, rows_of(h, HALF), :] = state.astype(F32)
            result = intra + dot(state, query, 1, 0)
            out[which, rows_of(h, HALF), :] = result
            sums_of[which][0] = sums_of[which][0] + fold(result * result)
            sums_of[which][1] = sums_of[which][1] + fold(weighted * result)
    odd = odd_of(mixing, BLOCK)
    mine, other = ([jnp.sum(part, axis=0, keepdims=True) for part in parts] for parts in sums_of)
    even_block = [jnp.where(odd, b, a) for a, b in zip(mine, other)]
    odd_block = [jnp.where(odd, a, b) for a, b in zip(mine, other)]
    both = jnp.concatenate(even_block + odd_block, axis=0)
    for peer in range(sums.shape[0]):
        sums[peer] = both


def pack_kernel(grad_t, held, exchange):
    exchange[:, 0:BLOCK] = grad_t[1].astype(F32)
    exchange[:, BLOCK:BLOCK + HD] = held[1]


def grad_kernel(mixing, sums, out, query_t, intra_t, weighted_t, partner, total, base, grad_t):
    odd = odd_of(mixing, BLOCK)
    count = query_t.shape[0] // HD
    first = mixing[7:8, 0:HD] > 0.5
    chips, one, width = total.shape
    wide = width // count
    share = wide // HD
    summed = jnp.sum(sums[...], axis=0)
    even_block, odd_block = summed[0:2], summed[2:4]
    scales = []
    for block in (jnp.where(odd, odd_block, even_block), jnp.where(odd, even_block, odd_block)):
        inverse = lax.rsqrt(block[0:1] / (HEADS * HD) + epsilon)
        scales.append((inverse, inverse * inverse * inverse * block[1:2] / (HEADS * HD)))
    for h in range(count):
        own, coming = (row[:, h * wide:h * wide + HD] for row in factors(mixing, True)[:2])
        terms = []
        for which, (query, intra, weighted) in enumerate(blocks_of(h, count, query_t, intra_t, weighted_t, partner)):
            inverse, factor = scales[which]
            grad = (weighted * inverse - out[which, rows_of(h, HALF), :] * factor).astype(BF16)
            grad_t[which, rows_of(h, HALF), :] = grad
            terms.append(dot(grad, query, 1, 1))
        put_half(base, h, jnp.where(first, terms[0], terms[1]))
        joined = own * terms[0] + coming * terms[1]
        for r in range(share):
            total[:, 0, lanes_of(h * share + r)] = joined[r * chips:(r + 1) * chips]


def local_kernel(rows, mixing, keys, values, grad_t, held, exchange, query_grad, back_attn, whole_grad):
    for h in range(keys.shape[1] // HD):
        place = lax.broadcasted_iota(jnp.int32, (1, BLOCK), 1).astype(F32)
        grad = whole(grad_t[0, rows_of(h, HALF), :].astype(F32), exchange[rows_of(h, HALF), 0:BLOCK], odd_of(mixing, BLOCK))
        state = whole(held[0, rows_of(h, HALF), :], exchange[rows_of(h, HALF), BLOCK:BLOCK + HD], odd_of(mixing))
        grad_dec = (grad * jnp.exp(-rows[h:h + 1, :] * (place + 1.0))).astype(BF16)
        grad = grad.astype(BF16)
        whole_grad[rows_of(h, HD), :] = grad
        mask = mask_of(rows[h:h + 1, :], decay_in_of(short(rows, h)))
        back = (dot(grad, head(values, h), 0, 1) * mask).astype(BF16)
        back_attn[h] = back
        query_grad[:, lanes_of(h)] = (
            dot(back, head(keys, h), 1, 0) + dot(grad_dec, state.astype(BF16), 0, 0)).astype(BF16)


def parts_kernel(queries, attn, back_attn, whole_grad, key_part, value_part):
    for h in range(attn.shape[0]):
        key_part[:, lanes_of(h)] = dot(back_attn[h], head(queries, h), 0, 0)
        value_part[:, lanes_of(h)] = dot(attn[h], whole_grad[rows_of(h, HD), :], 0, 1)


def last_kernel(rows, mixing, keys, values, mine, other, key_part, value_part, query_out,
                query_grad, key_grad, value_grad, key_out, value_out, sems):
    odd = odd_of(mixing)
    copies = [pltpu.make_async_copy(query_out, query_grad, sems.at[2 * (keys.shape[1] // HD)])]
    copies[0].start()
    for h in range(keys.shape[1] // HD):
        later = get_state(mine, other, h, odd)
        decay_out = decay_out_of(short(rows, h))
        value_dec = scaled(head(values, h), decay_out)
        key_dec = scaled(head(keys, h), decay_out)
        key_out[:, lanes_of(h)] = (head(key_part, h) + dot(value_dec, later, 1, 0)).astype(BF16)
        value_out[:, lanes_of(h)] = (head(value_part, h) + dot(key_dec, later, 1, 1)).astype(BF16)
        for which, (source, target) in enumerate(((key_out, key_grad), (value_out, value_grad))):
            copies.append(pltpu.make_async_copy(
                source.at[:, lanes_of(h)], target.at[:, lanes_of(h)], sems.at[2 * h + which]))
            copies[-1].start()
    for copy in copies:
        copy.wait()


def call(body, name, args, shapes, specs=None, scratch=(), flops=0, into=VMEM):
    outs = [jax.ShapeDtypeStruct(shape, kind) for shape, kind in shapes]
    moved = sum(a.size * a.dtype.itemsize for a in args)
    return pl.pallas_call(
        body,
        out_shape=outs if len(outs) > 1 else outs[0],
        in_specs=specs or [VMEM] * len(args),
        out_specs=[into] * len(outs) if len(outs) > 1 else into,
        scratch_shapes=list(scratch),
        compiler_params=pltpu.CompilerParams(vmem_limit_bytes=16 * 1024 * 1024),
        cost_estimate=pl.CostEstimate(flops=flops, bytes_accessed=moved, transcendentals=0),
        name=name,
    )(*args)


def per_device(queries, keys, values, out_grad, rates, gain):
    tokens, width = queries.shape
    count = rates.shape[0]
    chips = lax.axis_size("ctx") // 2
    ranks = lax.axis_size("head")
    lanes = count * HD * HALF // chips
    half, flat, rows_half = ((chips, lanes), F32), ((chips, 1, lanes), F32), ((count * HALF, BLOCK), F32)
    gain = gain.reshape(1, width)
    wide16, wide32 = ((BLOCK, width), BF16), ((BLOCK, width), F32)
    square = ((count, BLOCK, BLOCK), BF16)
    unit = BLOCK * BLOCK * width
    partners = [(i, i ^ 1) for i in range(2 * chips)]
    rings = [[2 * i + c for i in range(chips)] for c in range(2)]
    towers = [[(2 * i + c) * ranks + y for c in range(2) for y in range(ranks)] for i in range(chips)]

    def swap(array):
        return lax.ppermute(array, "ctx", partners)

    def spread_out(array):
        return lax.all_to_all(array, "ctx", 0, 0, tiled=True, axis_index_groups=rings)

    keep, send, rows, mixing, key_in, value_in, query_in, grad_in = call(
        kv_kernel, "kv", [pltpu.with_memory_space_constraint(a, pltpu.HBM) for a in (rates, keys, values, queries, out_grad)],
        [half, half, ((8, BLOCK), F32), ((8, lanes), F32)] + [wide16] * 4,
        specs=[HBM] * 5,
        scratch=[pltpu.SMEM((count,), F32), pltpu.VMEM((BLOCK, width), F32),
                 pltpu.SemaphoreType.DMA((5,))])
    got = swap(send)
    attn, query_t, intra_t, weighted_t, partner = call(
        intra_kernel, "intra", [rows, mixing, query_in, key_in, value_in, grad_in, gain],
        [square, ((width, BLOCK), BF16), rows_half, rows_half, ((2 * width, BLOCK), F32)], flops=4 * unit)
    got, partner = lax.optimization_barrier((got, partner))
    total = call(functools.partial(join_kernel, False), "join", [mixing, keep, got], [flat])
    total = spread_out(total)
    prefix = call(functools.partial(scan_kernel, False), "scan", [rows, total], [flat])
    prefix, partner = lax.optimization_barrier((prefix, partner))
    partner = swap(partner)
    prefix = spread_out(prefix)
    shared = [query_t, intra_t, weighted_t, partner]
    out, held, sums = call(
        out_kernel, "out", [mixing, keep, got, prefix] + shared,
        [((2, count * HALF, BLOCK), F32), ((2, count * HALF, HD), F32), ((2 * ranks, 4, BLOCK), F32)])
    sums = lax.all_to_all(sums, ("ctx", "head"), 0, 0, tiled=True, axis_index_groups=towers)
    total, base, grad_t = call(
        grad_kernel, "grad", [mixing, sums, out] + shared,
        [flat, half, ((2, count * HALF, BLOCK), BF16)])
    total = spread_out(total)
    exchange = swap(call(pack_kernel, "pack", [grad_t, held], [((count * HALF, BLOCK + HD), F32)], flops=4 * unit))
    prefix = spread_out(call(functools.partial(scan_kernel, True), "scan", [rows, total], [flat]))
    mine, other = call(
        functools.partial(spread_kernel, True), "spread", [mixing, base, prefix], [half, half])
    tied, other = lax.optimization_barrier((rows, other))
    other = swap(other)
    query_grad, back_attn, whole_grad = call(
        local_kernel, "local", [tied, mixing, keys, values, grad_t, held, exchange],
        [wide16, square, ((width, BLOCK), BF16)], flops=4 * unit)
    key_part, value_part = call(
        parts_kernel, "parts", [queries, attn, back_attn, whole_grad], [wide32, wide32], flops=4 * unit)
    other, key_part, value_part = lax.optimization_barrier((other, key_part, value_part))
    outs = call(
        last_kernel, "last", [rows, mixing, keys, values, mine, other, key_part, value_part, query_grad],
        [wide16] * 3,
        scratch=[pltpu.VMEM((BLOCK, width), BF16), pltpu.VMEM((BLOCK, width), BF16),
                 pltpu.SemaphoreType.DMA((2 * count + 1,))],
        into=HBM)
    return tuple(outs)


def solution(mesh):
    spec = P("ctx", "head")
    return jax.shard_map(
        per_device, mesh=mesh, in_specs=(spec, spec, spec, spec, P("head"), P("head")),
        out_specs=(spec, spec, spec), check_vma=False)
```

```python
import functools

import jax
import jax.numpy as jnp
from jax import lax
from jax.experimental import pallas as pl
from jax.experimental.pallas import tpu as pltpu
from jax.sharding import PartitionSpec as P

HD = 128
HEADS = 40
BLOCK = 256
epsilon = 1e-05

HALF = HD // 2
F32 = jnp.float32
BF16 = jnp.bfloat16
VMEM = pl.BlockSpec(memory_space=pltpu.VMEM)
HBM = pl.BlockSpec(memory_space=pltpu.HBM)


def dot(a, b, ca, cb):
    return lax.dot_general(a, b, (((ca,), (cb,)), ((), ())), preferred_element_type=F32)


def lanes_of(h):
    return slice(h * HD, (h + 1) * HD)


def head(ref, h):
    return ref[:, lanes_of(h)]


def decay_in_of(rate):
    place = lax.broadcasted_iota(jnp.int32, (8, HD), 0).astype(F32)
    table = jnp.exp(-rate * (place + 1.0))
    while table.shape[0] < BLOCK:
        step = jnp.exp(jnp.full((1, HD), -float(table.shape[0]), F32) * rate)
        table = jnp.concatenate([table, table * step], axis=0)
    return table


def decay_out_of(rate):
    place = lax.broadcasted_iota(jnp.int32, (8, HD), 0).astype(F32)
    table = jnp.exp(-rate * (7.0 - place))
    while table.shape[0] < BLOCK:
        step = jnp.exp(jnp.full((1, HD), -float(table.shape[0]), F32) * rate)
        table = jnp.concatenate([table * step, table], axis=0)
    return table


def mask_of(rates, decay_in):
    row = lax.broadcasted_iota(jnp.int32, (BLOCK, BLOCK), 0)
    col = lax.broadcasted_iota(jnp.int32, (BLOCK, BLOCK), 1)
    place = lax.broadcasted_iota(jnp.int32, (1, BLOCK), 1).astype(F32)
    growth = jnp.exp(rates * (place + 1.0))
    both = jnp.concatenate([decay_in, decay_in], axis=1) * growth
    return jnp.where(row >= col, both, 0.0)


def short(rows, h):
    return rows[h:h + 1, 0:HD]


def scaled(array, scale):
    return (array.astype(F32) * scale).astype(BF16)


def put_halves(keep, send, h, state, odd):
    chips = keep.shape[0]
    share = HD // 2 // chips
    low, high = state[:HD // 2], state[HD // 2:]
    mine, other = jnp.where(odd, high, low), jnp.where(odd, low, high)
    for r in range(share):
        lane = (h * share + r) * HD
        keep[:, lane:lane + HD] = mine[r * chips:(r + 1) * chips]
        send[:, lane:lane + HD] = other[r * chips:(r + 1) * chips]


def put_half(ref, h, state):
    chips = ref.shape[0]
    share = HD // 2 // chips
    for r in range(share):
        lane = (h * share + r) * HD
        ref[:, lane:lane + HD] = state[r * chips:(r + 1) * chips]


def get_half(ref, h):
    chips = ref.shape[0]
    share = HD // 2 // chips
    return jnp.concatenate([ref[:, lanes_of(h * share + r)] for r in range(share)], axis=0)


def rows_of(h, size, start=0):
    return slice(start + h * size, start + (h + 1) * size)


def whole(mine, other, odd):
    low, high = jnp.where(odd, other, mine), jnp.where(odd, mine, other)
    return jnp.concatenate([low, high], axis=0)


def get_state(mine, other, h, odd):
    return whole(get_half(mine, h), get_half(other, h), odd).astype(BF16)


def kv_kernel(rates, keys, values, queries, out_grad, keep, send, rows, mixing, key_in, value_in, query_in, grad_in,
              rate, decays, sems):
    count = rates.shape[0]
    odd = lax.rem(lax.axis_index("ctx"), 2) == 1
    pairs = ((rates, rate), (keys, key_in), (values, value_in), (queries, query_in), (out_grad, grad_in))
    copies = [pltpu.make_async_copy(source, target, sems.at[i]) for i, (source, target) in enumerate(pairs)]
    for copy in copies:
        copy.start()
    copies[0].wait()
    wide = mixing.shape[1] // count
    index = lax.broadcasted_iota(jnp.int32, (8, wide), 0)
    for h in range(count):
        rows[h:h + 1, :] = jnp.full((1, BLOCK), rate[h], F32)
        decay = jnp.exp(jnp.full((8, wide), -rate[h] * BLOCK, F32))
        place = lax.rem(index, 4)
        later = index >= 4
        first = later == odd
        on_first = jnp.where(place == 0, decay, jnp.where(place == 2, 0.0, 1.0))
        on_second = jnp.where(place == 1, decay, jnp.where(place == 3, 0.0, 1.0))
        mixing[:, h * wide:(h + 1) * wide] = jnp.where(first, on_first, on_second)
        decays[:, lanes_of(h)] = decay_out_of(jnp.full((1, HD), rate[h], F32))
    copies[1].wait()
    copies[2].wait()
    for h in range(count):
        key_dec = scaled(head(key_in, h), head(decays, h))
        put_halves(keep, send, h, dot(head(value_in, h), key_dec, 0, 0), odd)
    copies[3].wait()
    copies[4].wait()


def odd_of(mixing, width=HD):
    return mixing[2:3, 0:width] > 0.5


def intra_kernel(rows, mixing, queries, keys, values, out_grad, gain, attn, query_t, intra_t, weighted_t, partner):
    odd = odd_of(mixing, BLOCK)
    count = queries.shape[1] // HD
    for h in range(count):
        decay_in = decay_in_of(short(rows, h))
        scores = dot(head(queries, h), head(keys, h), 1, 1)
        weights = (scores * mask_of(rows[h:h + 1, :], decay_in)).astype(BF16)
        attn[h] = weights
        query_dec = scaled(head(queries, h), decay_in).astype(F32).T
        query_t[rows_of(h, HD), :] = query_dec.astype(BF16)
        partner[rows_of(h, HD), :] = query_dec
        intra = dot(head(values, h), weights, 0, 1)
        weighted = (head(out_grad, h).astype(F32) * head(gain, h)).T
        start = count * HD
        for array, target in ((intra, intra_t), (weighted, weighted_t)):
            low, high = array[:HALF], array[HALF:]
            target[rows_of(h, HALF), :] = jnp.where(odd, high, low)
            partner[rows_of(h, HALF, start), :] = jnp.where(odd, low, high)
            start += count * HALF


def factors(mixing, backward):
    return [mixing[i:i + 1, :] for i in range(4 * backward, 4 * backward + 4)]


def join_kernel(backward, mixing, keep, got, total):
    own, coming = factors(mixing, backward)[:2]
    total[:, 0, :] = own * keep[...] + coming * got[...]


def spread_kernel(backward, mixing, base, prefix, mine, other):
    own, coming, add_mine, add_other = factors(mixing, backward)
    incoming = prefix[:, 0, :]
    other[...] = own * incoming + add_other * base[...]
    mine[...] = coming * incoming + add_mine * base[...]


def scan_kernel(backward, rows, totals, prefix):
    chips, one, width = totals.shape
    count = width * chips * 2 // HD // HD
    wide = width // count
    row = lax.broadcasted_iota(jnp.int32, (chips, chips), 0)
    col = lax.broadcasted_iota(jnp.int32, (chips, chips), 1)
    far = ((col - row - 1) if backward else (row - col - 1)).astype(F32)
    for h in range(count):
        lanes = slice(h * wide, (h + 1) * wide)
        rate = rows[h:h + 1, 0:chips]
        weight = jnp.where(far >= 0.0, jnp.exp(-(rate * (2.0 * BLOCK)) * jnp.maximum(far, 0.0)), 0.0)
        prefix[:, 0, lanes] = lax.dot_general(
            weight, totals[:, 0, lanes], (((1,), (0,)), ((), ())),
            precision=lax.Precision.HIGHEST, preferred_element_type=F32)


def fold(array):
    return jnp.sum(array.reshape(HALF // 8, 8, BLOCK), axis=0)


def blocks_of(h, count, query_t, intra_t, weighted_t, partner):
    mine = (query_t[rows_of(h, HD), :], intra_t[rows_of(h, HALF), :], weighted_t[rows_of(h, HALF), :])
    other = (partner[rows_of(h, HD), :].astype(BF16), partner[rows_of(h, HALF, count * HD), :],
             partner[rows_of(h, HALF, count * (HD + HALF)), :])
    return mine, other


def out_kernel(mixing, keep, got, prefix, query_t, intra_t, weighted_t, partner, out, held, sums):
    chips, width = keep.shape
    count = query_t.shape[0] // HD
    wide = width // count
    share = wide // HD
    sums_of = [[jnp.zeros((8, BLOCK), F32) for _ in range(2)] for _ in range(2)]
    for h in range(count):
        own, coming, add_mine, add_other = (row[:, h * wide:h * wide + HD] for row in factors(mixing, False))
        incoming = jnp.concatenate([prefix[:, 0, lanes_of(h * share + r)] for r in range(share)], axis=0)
        states = (coming * incoming + add_mine * get_half(got, h), own * incoming + add_other * get_half(keep, h))
        for which, (query, intra, weighted) in enumerate(blocks_of(h, count, query_t, intra_t, weighted_t, partner)):
            state = states[which].astype(BF16)
            held[which, rows_of(h, HALF), :] = state.astype(F32)
            result = intra + dot(state, query, 1, 0)
            out[which, rows_of(h, HALF), :] = result
            sums_of[which][0] = sums_of[which][0] + fold(result * result)
            sums_of[which][1] = sums_of[which][1] + fold(weighted * result)
    odd = odd_of(mixing, BLOCK)
    mine, other = ([jnp.sum(part, axis=0, keepdims=True) for part in parts] for parts in sums_of)
    even_block = [jnp.where(odd, b, a) for a, b in zip(mine, other)]
    odd_block = [jnp.where(odd, a, b) for a, b in zip(mine, other)]
    both = jnp.concatenate(even_block + odd_block, axis=0)
    for peer in range(sums.shape[0]):
        sums[peer] = both


def pack_kernel(grad_t, held, exchange):
    exchange[:, 0:BLOCK] = grad_t[1].astype(F32)
    exchange[:, BLOCK:BLOCK + HD] = held[1]


def grad_kernel(mixing, sums, out, query_t, intra_t, weighted_t, partner, total, base, grad_t):
    odd = odd_of(mixing, BLOCK)
    count = query_t.shape[0] // HD
    first = mixing[7:8, 0:HD] > 0.5
    chips, one, width = total.shape
    wide = width // count
    share = wide // HD
    summed = jnp.sum(sums[...], axis=0)
    even_block, odd_block = summed[0:2], summed[2:4]
    scales = []
    for block in (jnp.where(odd, odd_block, even_block), jnp.where(odd, even_block, odd_block)):
        inverse = lax.rsqrt(block[0:1] / (HEADS * HD) + epsilon)
        scales.append((inverse, inverse * inverse * inverse * block[1:2] / (HEADS * HD)))
    for h in range(count):
        own, coming = (row[:, h * wide:h * wide + HD] for row in factors(mixing, True)[:2])
        terms = []
        for which, (query, intra, weighted) in enumerate(blocks_of(h, count, query_t, intra_t, weighted_t, partner)):
            inverse, factor = scales[which]
            grad = (weighted * inverse - out[which, rows_of(h, HALF), :] * factor).astype(BF16)
            grad_t[which, rows_of(h, HALF), :] = grad
            terms.append(dot(grad, query, 1, 1))
        put_half(base, h, jnp.where(first, terms[0], terms[1]))
        joined = own * terms[0] + coming * terms[1]
        for r in range(share):
            total[:, 0, lanes_of(h * share + r)] = joined[r * chips:(r + 1) * chips]


def local_kernel(rows, mixing, keys, values, grad_t, held, exchange, query_grad, back_attn, whole_grad):
    for h in range(keys.shape[1] // HD):
        place = lax.broadcasted_iota(jnp.int32, (1, BLOCK), 1).astype(F32)
        grad = whole(grad_t[0, rows_of(h, HALF), :].astype(F32), exchange[rows_of(h, HALF), 0:BLOCK], odd_of(mixing, BLOCK))
        state = whole(held[0, rows_of(h, HALF), :], exchange[rows_of(h, HALF), BLOCK:BLOCK + HD], odd_of(mixing))
        grad_dec = (grad * jnp.exp(-rows[h:h + 1, :] * (place + 1.0))).astype(BF16)
        grad = grad.astype(BF16)
        whole_grad[rows_of(h, HD), :] = grad
        mask = mask_of(rows[h:h + 1, :], decay_in_of(short(rows, h)))
        back = (dot(grad, head(values, h), 0, 1) * mask).astype(BF16)
        back_attn[h] = back
        query_grad[:, lanes_of(h)] = (
            dot(back, head(keys, h), 1, 0) + dot(grad_dec, state.astype(BF16), 0, 0)).astype(BF16)


def parts_kernel(queries, attn, back_attn, whole_grad, key_part, value_part):
    for h in range(attn.shape[0]):
        key_part[:, lanes_of(h)] = dot(back_attn[h], head(queries, h), 0, 0)
        value_part[:, lanes_of(h)] = dot(attn[h], whole_grad[rows_of(h, HD), :], 0, 1)


def last_kernel(rows, mixing, keys, values, mine, other, key_part, value_part, query_out,
                query_grad, key_grad, value_grad, key_out, value_out, sems):
    odd = odd_of(mixing)
    copies = [pltpu.make_async_copy(query_out, query_grad, sems.at[2 * (keys.shape[1] // HD)])]
    copies[0].start()
    for h in range(keys.shape[1] // HD):
        later = get_state(mine, other, h, odd)
        decay_out = decay_out_of(short(rows, h))
        value_dec = scaled(head(values, h), decay_out)
        key_dec = scaled(head(keys, h), decay_out)
        key_out[:, lanes_of(h)] = (head(key_part, h) + dot(value_dec, later, 1, 0)).astype(BF16)
        value_out[:, lanes_of(h)] = (head(value_part, h) + dot(key_dec, later, 1, 1)).astype(BF16)
        for which, (source, target) in enumerate(((key_out, key_grad), (value_out, value_grad))):
            copies.append(pltpu.make_async_copy(
                source.at[:, lanes_of(h)], target.at[:, lanes_of(h)], sems.at[2 * h + which]))
            copies[-1].start()
    for copy in copies:
        copy.wait()


def call(body, name, args, shapes, specs=None, scratch=(), flops=0, into=VMEM):
    outs = [jax.ShapeDtypeStruct(shape, kind) for shape, kind in shapes]
    moved = sum(a.size * a.dtype.itemsize for a in args)
    return pl.pallas_call(
        body,
        out_shape=outs if len(outs) > 1 else outs[0],
        in_specs=specs or [VMEM] * len(args),
        out_specs=[into] * len(outs) if len(outs) > 1 else into,
        scratch_shapes=list(scratch),
        compiler_params=pltpu.CompilerParams(vmem_limit_bytes=16 * 1024 * 1024),
        cost_estimate=pl.CostEstimate(flops=flops, bytes_accessed=moved, transcendentals=0),
        name=name,
    )(*args)


def per_device(queries, keys, values, out_grad, rates, gain):
    tokens, width = queries.shape
    count = rates.shape[0]
    chips = lax.axis_size("ctx") // 2
    ranks = lax.axis_size("head")
    lanes = count * HD * HALF // chips
    half, flat, rows_half = ((chips, lanes), F32), ((chips, 1, lanes), F32), ((count * HALF, BLOCK), F32)
    gain = gain.reshape(1, width)
    wide16, wide32 = ((BLOCK, width), BF16), ((BLOCK, width), F32)
    square = ((count, BLOCK, BLOCK), BF16)
    unit = BLOCK * BLOCK * width
    partners = [(i, i ^ 1) for i in range(2 * chips)]
    rings = [[2 * i + c for i in range(chips)] for c in range(2)]
    towers = [[(2 * i + c) * ranks + y for c in range(2) for y in range(ranks)] for i in range(chips)]

    def swap(array):
        return lax.ppermute(array, "ctx", partners)

    def spread_out(array):
        return lax.all_to_all(array, "ctx", 0, 0, tiled=True, axis_index_groups=rings)

    keep, send, rows, mixing, key_in, value_in, query_in, grad_in = call(
        kv_kernel, "kv", [pltpu.with_memory_space_constraint(a, pltpu.HBM) for a in (rates, keys, values, queries, out_grad)],
        [half, half, ((8, BLOCK), F32), ((8, lanes), F32)] + [wide16] * 4,
        specs=[HBM] * 5,
        scratch=[pltpu.SMEM((count,), F32), pltpu.VMEM((BLOCK, width), F32),
                 pltpu.SemaphoreType.DMA((5,))])
    got = swap(send)
    attn, query_t, intra_t, weighted_t, partner = call(
        intra_kernel, "intra", [rows, mixing, query_in, key_in, value_in, grad_in, gain],
        [square, ((width, BLOCK), BF16), rows_half, rows_half, ((2 * width, BLOCK), F32)], flops=4 * unit)
    got, partner = lax.optimization_barrier((got, partner))
    total = call(functools.partial(join_kernel, False), "join", [mixing, keep, got], [flat])
    total, partner = lax.optimization_barrier((total, partner))
    partner = swap(partner)
    total = spread_out(total)
    prefix = spread_out(call(functools.partial(scan_kernel, False), "scan", [rows, total], [flat]))
    shared = [query_t, intra_t, weighted_t, partner]
    out, held, sums = call(
        out_kernel, "out", [mixing, keep, got, prefix] + shared,
        [((2, count * HALF, BLOCK), F32), ((2, count * HALF, HD), F32), ((2 * ranks, 4, BLOCK), F32)])
    sums = lax.all_to_all(sums, ("ctx", "head"), 0, 0, tiled=True, axis_index_groups=towers)
    total, base, grad_t = call(
        grad_kernel, "grad", [mixing, sums, out] + shared,
        [flat, half, ((2, count * HALF, BLOCK), BF16)])
    total = spread_out(total)
    exchange = swap(call(pack_kernel, "pack", [grad_t, held], [((count * HALF, BLOCK + HD), F32)], flops=4 * unit))
    prefix = spread_out(call(functools.partial(scan_kernel, True), "scan", [rows, total], [flat]))
    mine, other = call(
        functools.partial(spread_kernel, True), "spread", [mixing, base, prefix], [half, half])
    tied, other = lax.optimization_barrier((rows, other))
    other = swap(other)
    query_grad, back_attn, whole_grad = call(
        local_kernel, "local", [tied, mixing, keys, values, grad_t, held, exchange],
        [wide16, square, ((width, BLOCK), BF16)], flops=4 * unit)
    key_part, value_part = call(
        parts_kernel, "parts", [queries, attn, back_attn, whole_grad], [wide32, wide32], flops=4 * unit)
    other, key_part, value_part = lax.optimization_barrier((other, key_part, value_part))
    outs = call(
        last_kernel, "last", [rows, mixing, keys, values, mine, other, key_part, value_part, query_grad],
        [wide16] * 3,
        scratch=[pltpu.VMEM((BLOCK, width), BF16), pltpu.VMEM((BLOCK, width), BF16),
                 pltpu.SemaphoreType.DMA((2 * count + 1,))],
        into=HBM)
    return tuple(outs)


def solution(mesh):
    spec = P("ctx", "head")
    return jax.shard_map(
        per_device, mesh=mesh, in_specs=(spec, spec, spec, spec, P("head"), P("head")),
        out_specs=(spec, spec, spec), check_vma=False)
```

```python
import functools

import jax
import jax.numpy as jnp
from jax import lax
from jax.experimental import pallas as pl
from jax.experimental.pallas import tpu as pltpu
from jax.sharding import PartitionSpec as P

HD = 128
HEADS = 40
BLOCK = 256
epsilon = 1e-05

HALF = HD // 2
F32 = jnp.float32
BF16 = jnp.bfloat16
VMEM = pl.BlockSpec(memory_space=pltpu.VMEM)
HBM = pl.BlockSpec(memory_space=pltpu.HBM)


def dot(a, b, ca, cb):
    return lax.dot_general(a, b, (((ca,), (cb,)), ((), ())), preferred_element_type=F32)


def lanes_of(h):
    return slice(h * HD, (h + 1) * HD)


def head(ref, h):
    return ref[:, lanes_of(h)]


def decay_in_of(rate):
    place = lax.broadcasted_iota(jnp.int32, (8, HD), 0).astype(F32)
    table = jnp.exp(-rate * (place + 1.0))
    while table.shape[0] < BLOCK:
        step = jnp.exp(jnp.full((1, HD), -float(table.shape[0]), F32) * rate)
        table = jnp.concatenate([table, table * step], axis=0)
    return table


def decay_out_of(rate):
    place = lax.broadcasted_iota(jnp.int32, (8, HD), 0).astype(F32)
    table = jnp.exp(-rate * (7.0 - place))
    while table.shape[0] < BLOCK:
        step = jnp.exp(jnp.full((1, HD), -float(table.shape[0]), F32) * rate)
        table = jnp.concatenate([table * step, table], axis=0)
    return table


def mask_of(rates, decay_in):
    row = lax.broadcasted_iota(jnp.int32, (BLOCK, BLOCK), 0)
    col = lax.broadcasted_iota(jnp.int32, (BLOCK, BLOCK), 1)
    place = lax.broadcasted_iota(jnp.int32, (1, BLOCK), 1).astype(F32)
    growth = jnp.exp(rates * (place + 1.0))
    both = jnp.concatenate([decay_in, decay_in], axis=1) * growth
    return jnp.where(row >= col, both, 0.0)


def short(rows, h):
    return rows[h:h + 1, 0:HD]


def scaled(array, scale):
    return (array.astype(F32) * scale).astype(BF16)


def put_halves(keep, send, h, state, odd):
    chips = keep.shape[0]
    share = HD // 2 // chips
    low, high = state[:HD // 2], state[HD // 2:]
    mine, other = jnp.where(odd, high, low), jnp.where(odd, low, high)
    for r in range(share):
        lane = (h * share + r) * HD
        keep[:, lane:lane + HD] = mine[r * chips:(r + 1) * chips]
        send[:, lane:lane + HD] = other[r * chips:(r + 1) * chips]


def put_half(ref, h, state):
    chips = ref.shape[0]
    share = HD // 2 // chips
    for r in range(share):
        lane = (h * share + r) * HD
        ref[:, lane:lane + HD] = state[r * chips:(r + 1) * chips]


def get_half(ref, h):
    chips = ref.shape[0]
    share = HD // 2 // chips
    return jnp.concatenate([ref[:, lanes_of(h * share + r)] for r in range(share)], axis=0)


def rows_of(h, size, start=0):
    return slice(start + h * size, start + (h + 1) * size)


def whole(mine, other, odd):
    low, high = jnp.where(odd, other, mine), jnp.where(odd, mine, other)
    return jnp.concatenate([low, high], axis=0)


def get_state(mine, other, h, odd):
    return whole(get_half(mine, h), get_half(other, h), odd).astype(BF16)


def kv_kernel(rates, keys, values, queries, out_grad, keep, send, rows, mixing, key_in, value_in, query_in, grad_in,
              rate, decays, sems):
    count = rates.shape[0]
    odd = lax.rem(lax.axis_index("ctx"), 2) == 1
    pairs = ((rates, rate), (keys, key_in), (values, value_in), (queries, query_in), (out_grad, grad_in))
    copies = [pltpu.make_async_copy(source, target, sems.at[i]) for i, (source, target) in enumerate(pairs)]
    for copy in copies:
        copy.start()
    copies[0].wait()
    wide = mixing.shape[1] // count
    index = lax.broadcasted_iota(jnp.int32, (8, wide), 0)
    for h in range(count):
        rows[h:h + 1, :] = jnp.full((1, BLOCK), rate[h], F32)
        decay = jnp.exp(jnp.full((8, wide), -rate[h] * BLOCK, F32))
        place = lax.rem(index, 4)
        later = index >= 4
        first = later == odd
        on_first = jnp.where(place == 0, decay, jnp.where(place == 2, 0.0, 1.0))
        on_second = jnp.where(place == 1, decay, jnp.where(place == 3, 0.0, 1.0))
        mixing[:, h * wide:(h + 1) * wide] = jnp.where(first, on_first, on_second)
        decays[:, lanes_of(h)] = decay_out_of(jnp.full((1, HD), rate[h], F32))
    copies[1].wait()
    key_dec = [scaled(head(key_in, h), head(decays, h)) for h in range(count)]
    copies[2].wait()
    for h in range(count):
        put_halves(keep, send, h, dot(head(value_in, h), key_dec[h], 0, 0), odd)
    copies[3].wait()
    copies[4].wait()


def odd_of(mixing, width=HD):
    return mixing[2:3, 0:width] > 0.5


def intra_kernel(rows, mixing, queries, keys, values, out_grad, gain, attn, query_t, intra_t, weighted_t, partner):
    odd = odd_of(mixing, BLOCK)
    count = queries.shape[1] // HD
    for h in range(count):
        decay_in = decay_in_of(short(rows, h))
        scores = dot(head(queries, h), head(keys, h), 1, 1)
        weights = (scores * mask_of(rows[h:h + 1, :], decay_in)).astype(BF16)
        attn[h] = weights
        query_dec = scaled(head(queries, h), decay_in).astype(F32).T
        query_t[rows_of(h, HD), :] = query_dec.astype(BF16)
        partner[rows_of(h, HD), :] = query_dec
        intra = dot(head(values, h), weights, 0, 1)
        weighted = (head(out_grad, h).astype(F32) * head(gain, h)).T
        start = count * HD
        for array, target in ((intra, intra_t), (weighted, weighted_t)):
            low, high = array[:HALF], array[HALF:]
            target[rows_of(h, HALF), :] = jnp.where(odd, high, low)
            partner[rows_of(h, HALF, start), :] = jnp.where(odd, low, high)
            start += count * HALF


def factors(mixing, backward):
    return [mixing[i:i + 1, :] for i in range(4 * backward, 4 * backward + 4)]


def join_kernel(backward, mixing, keep, got, total):
    own, coming = factors(mixing, backward)[:2]
    total[:, 0, :] = own * keep[...] + coming * got[...]


def spread_kernel(backward, mixing, base, prefix, mine, other):
    own, coming, add_mine, add_other = factors(mixing, backward)
    incoming = prefix[:, 0, :]
    other[...] = own * incoming + add_other * base[...]
    mine[...] = coming * incoming + add_mine * base[...]


def scan_kernel(backward, rows, totals, prefix):
    chips, one, width = totals.shape
    count = width * chips * 2 // HD // HD
    wide = width // count
    row = lax.broadcasted_iota(jnp.int32, (chips, chips), 0)
    col = lax.broadcasted_iota(jnp.int32, (chips, chips), 1)
    far = ((col - row - 1) if backward else (row - col - 1)).astype(F32)
    for h in range(count):
        lanes = slice(h * wide, (h + 1) * wide)
        rate = rows[h:h + 1, 0:chips]
        weight = jnp.where(far >= 0.0, jnp.exp(-(rate * (2.0 * BLOCK)) * jnp.maximum(far, 0.0)), 0.0)
        prefix[:, 0, lanes] = lax.dot_general(
            weight, totals[:, 0, lanes], (((1,), (0,)), ((), ())),
            precision=lax.Precision.HIGHEST, preferred_element_type=F32)


def fold(array):
    return jnp.sum(array.reshape(HALF // 8, 8, BLOCK), axis=0)


def blocks_of(h, count, query_t, intra_t, weighted_t, partner):
    mine = (query_t[rows_of(h, HD), :], intra_t[rows_of(h, HALF), :], weighted_t[rows_of(h, HALF), :])
    other = (partner[rows_of(h, HD), :].astype(BF16), partner[rows_of(h, HALF, count * HD), :],
             partner[rows_of(h, HALF, count * (HD + HALF)), :])
    return mine, other


def out_kernel(mixing, keep, got, prefix, query_t, intra_t, weighted_t, partner, out, held, sums):
    chips, width = keep.shape
    count = query_t.shape[0] // HD
    wide = width // count
    share = wide // HD
    sums_of = [[jnp.zeros((8, BLOCK), F32) for _ in range(2)] for _ in range(2)]
    for h in range(count):
        own, coming, add_mine, add_other = (row[:, h * wide:h * wide + HD] for row in factors(mixing, False))
        incoming = jnp.concatenate([prefix[:, 0, lanes_of(h * share + r)] for r in range(share)], axis=0)
        states = (coming * incoming + add_mine * get_half(got, h), own * incoming + add_other * get_half(keep, h))
        for which, (query, intra, weighted) in enumerate(blocks_of(h, count, query_t, intra_t, weighted_t, partner)):
            state = states[which].astype(BF16)
            held[which, rows_of(h, HALF), :] = state.astype(F32)
            result = intra + dot(state, query, 1, 0)
            out[which, rows_of(h, HALF), :] = result
            sums_of[which][0] = sums_of[which][0] + fold(result * result)
            sums_of[which][1] = sums_of[which][1] + fold(weighted * result)
    odd = odd_of(mixing, BLOCK)
    mine, other = ([jnp.sum(part, axis=0, keepdims=True) for part in parts] for parts in sums_of)
    even_block = [jnp.where(odd, b, a) for a, b in zip(mine, other)]
    odd_block = [jnp.where(odd, a, b) for a, b in zip(mine, other)]
    both = jnp.concatenate(even_block + odd_block, axis=0)
    for peer in range(sums.shape[0]):
        sums[peer] = both


def pack_kernel(grad_t, held, exchange):
    exchange[:, 0:BLOCK] = grad_t[1].astype(F32)
    exchange[:, BLOCK:BLOCK + HD] = held[1]


def grad_kernel(mixing, sums, out, query_t, intra_t, weighted_t, partner, total, base, grad_t):
    odd = odd_of(mixing, BLOCK)
    count = query_t.shape[0] // HD
    first = mixing[7:8, 0:HD] > 0.5
    chips, one, width = total.shape
    wide = width // count
    share = wide // HD
    summed = jnp.sum(sums[...], axis=0)
    even_block, odd_block = summed[0:2], summed[2:4]
    scales = []
    for block in (jnp.where(odd, odd_block, even_block), jnp.where(odd, even_block, odd_block)):
        inverse = lax.rsqrt(block[0:1] / (HEADS * HD) + epsilon)
        scales.append((inverse, inverse * inverse * inverse * block[1:2] / (HEADS * HD)))
    for h in range(count):
        own, coming = (row[:, h * wide:h * wide + HD] for row in factors(mixing, True)[:2])
        terms = []
        for which, (query, intra, weighted) in enumerate(blocks_of(h, count, query_t, intra_t, weighted_t, partner)):
            inverse, factor = scales[which]
            grad = (weighted * inverse - out[which, rows_of(h, HALF), :] * factor).astype(BF16)
            grad_t[which, rows_of(h, HALF), :] = grad
            terms.append(dot(grad, query, 1, 1))
        put_half(base, h, jnp.where(first, terms[0], terms[1]))
        joined = own * terms[0] + coming * terms[1]
        for r in range(share):
            total[:, 0, lanes_of(h * share + r)] = joined[r * chips:(r + 1) * chips]


def local_kernel(rows, mixing, keys, values, grad_t, held, exchange, query_grad, back_attn, whole_grad):
    for h in range(keys.shape[1] // HD):
        place = lax.broadcasted_iota(jnp.int32, (1, BLOCK), 1).astype(F32)
        grad = whole(grad_t[0, rows_of(h, HALF), :].astype(F32), exchange[rows_of(h, HALF), 0:BLOCK], odd_of(mixing, BLOCK))
        state = whole(held[0, rows_of(h, HALF), :], exchange[rows_of(h, HALF), BLOCK:BLOCK + HD], odd_of(mixing))
        grad_dec = (grad * jnp.exp(-rows[h:h + 1, :] * (place + 1.0))).astype(BF16)
        grad = grad.astype(BF16)
        whole_grad[rows_of(h, HD), :] = grad
        mask = mask_of(rows[h:h + 1, :], decay_in_of(short(rows, h)))
        back = (dot(grad, head(values, h), 0, 1) * mask).astype(BF16)
        back_attn[h] = back
        query_grad[:, lanes_of(h)] = (
            dot(back, head(keys, h), 1, 0) + dot(grad_dec, state.astype(BF16), 0, 0)).astype(BF16)


def parts_kernel(queries, attn, back_attn, whole_grad, key_part, value_part):
    for h in range(attn.shape[0]):
        key_part[:, lanes_of(h)] = dot(back_attn[h], head(queries, h), 0, 0)
        value_part[:, lanes_of(h)] = dot(attn[h], whole_grad[rows_of(h, HD), :], 0, 1)


def last_kernel(rows, mixing, keys, values, mine, other, key_part, value_part, query_out,
                query_grad, key_grad, value_grad, key_out, value_out, sems):
    odd = odd_of(mixing)
    copies = [pltpu.make_async_copy(query_out, query_grad, sems.at[2 * (keys.shape[1] // HD)])]
    copies[0].start()
    for h in range(keys.shape[1] // HD):
        later = get_state(mine, other, h, odd)
        decay_out = decay_out_of(short(rows, h))
        value_dec = scaled(head(values, h), decay_out)
        key_dec = scaled(head(keys, h), decay_out)
        key_out[:, lanes_of(h)] = (head(key_part, h) + dot(value_dec, later, 1, 0)).astype(BF16)
        value_out[:, lanes_of(h)] = (head(value_part, h) + dot(key_dec, later, 1, 1)).astype(BF16)
        for which, (source, target) in enumerate(((key_out, key_grad), (value_out, value_grad))):
            copies.append(pltpu.make_async_copy(
                source.at[:, lanes_of(h)], target.at[:, lanes_of(h)], sems.at[2 * h + which]))
            copies[-1].start()
    for copy in copies:
        copy.wait()


def call(body, name, args, shapes, specs=None, scratch=(), flops=0, into=VMEM):
    outs = [jax.ShapeDtypeStruct(shape, kind) for shape, kind in shapes]
    moved = sum(a.size * a.dtype.itemsize for a in args)
    return pl.pallas_call(
        body,
        out_shape=outs if len(outs) > 1 else outs[0],
        in_specs=specs or [VMEM] * len(args),
        out_specs=[into] * len(outs) if len(outs) > 1 else into,
        scratch_shapes=list(scratch),
        compiler_params=pltpu.CompilerParams(vmem_limit_bytes=16 * 1024 * 1024),
        cost_estimate=pl.CostEstimate(flops=flops, bytes_accessed=moved, transcendentals=0),
        name=name,
    )(*args)


def per_device(queries, keys, values, out_grad, rates, gain):
    tokens, width = queries.shape
    count = rates.shape[0]
    chips = lax.axis_size("ctx") // 2
    ranks = lax.axis_size("head")
    lanes = count * HD * HALF // chips
    half, flat, rows_half = ((chips, lanes), F32), ((chips, 1, lanes), F32), ((count * HALF, BLOCK), F32)
    gain = gain.reshape(1, width)
    wide16, wide32 = ((BLOCK, width), BF16), ((BLOCK, width), F32)
    square = ((count, BLOCK, BLOCK), BF16)
    unit = BLOCK * BLOCK * width
    partners = [(i, i ^ 1) for i in range(2 * chips)]
    rings = [[2 * i + c for i in range(chips)] for c in range(2)]
    towers = [[(2 * i + c) * ranks + y for c in range(2) for y in range(ranks)] for i in range(chips)]

    def swap(array):
        return lax.ppermute(array, "ctx", partners)

    def spread_out(array):
        return lax.all_to_all(array, "ctx", 0, 0, tiled=True, axis_index_groups=rings)

    keep, send, rows, mixing, key_in, value_in, query_in, grad_in = call(
        kv_kernel, "kv", [pltpu.with_memory_space_constraint(a, pltpu.HBM) for a in (rates, keys, values, queries, out_grad)],
        [half, half, ((8, BLOCK), F32), ((8, lanes), F32)] + [wide16] * 4,
        specs=[HBM] * 5,
        scratch=[pltpu.SMEM((count,), F32), pltpu.VMEM((BLOCK, width), F32),
                 pltpu.SemaphoreType.DMA((5,))])
    got = swap(send)
    attn, query_t, intra_t, weighted_t, partner = call(
        intra_kernel, "intra", [rows, mixing, query_in, key_in, value_in, grad_in, gain],
        [square, ((width, BLOCK), BF16), rows_half, rows_half, ((2 * width, BLOCK), F32)], flops=4 * unit)
    got, partner = lax.optimization_barrier((got, partner))
    total = call(functools.partial(join_kernel, False), "join", [mixing, keep, got], [flat])
    total, partner = lax.optimization_barrier((total, partner))
    partner = swap(partner)
    total = spread_out(total)
    prefix = spread_out(call(functools.partial(scan_kernel, False), "scan", [rows, total], [flat]))
    shared = [query_t, intra_t, weighted_t, partner]
    out, held, sums = call(
        out_kernel, "out", [mixing, keep, got, prefix] + shared,
        [((2, count * HALF, BLOCK), F32), ((2, count * HALF, HD), F32), ((2 * ranks, 4, BLOCK), F32)])
    sums = lax.all_to_all(sums, ("ctx", "head"), 0, 0, tiled=True, axis_index_groups=towers)
    total, base, grad_t = call(
        grad_kernel, "grad", [mixing, sums, out] + shared,
        [flat, half, ((2, count * HALF, BLOCK), BF16)])
    total = spread_out(total)
    exchange = swap(call(pack_kernel, "pack", [grad_t, held], [((count * HALF, BLOCK + HD), F32)], flops=4 * unit))
    prefix = spread_out(call(functools.partial(scan_kernel, True), "scan", [rows, total], [flat]))
    mine, other = call(
        functools.partial(spread_kernel, True), "spread", [mixing, base, prefix], [half, half])
    tied, other = lax.optimization_barrier((rows, other))
    other = swap(other)
    query_grad, back_attn, whole_grad = call(
        local_kernel, "local", [tied, mixing, keys, values, grad_t, held, exchange],
        [wide16, square, ((width, BLOCK), BF16)], flops=4 * unit)
    key_part, value_part = call(
        parts_kernel, "parts", [queries, attn, back_attn, whole_grad], [wide32, wide32], flops=4 * unit)
    other, key_part, value_part = lax.optimization_barrier((other, key_part, value_part))
    outs = call(
        last_kernel, "last", [rows, mixing, keys, values, mine, other, key_part, value_part, query_grad],
        [wide16] * 3,
        scratch=[pltpu.VMEM((BLOCK, width), BF16), pltpu.VMEM((BLOCK, width), BF16),
                 pltpu.SemaphoreType.DMA((2 * count + 1,))],
        into=HBM)
    return tuple(outs)


def solution(mesh):
    spec = P("ctx", "head")
    return jax.shard_map(
        per_device, mesh=mesh, in_specs=(spec, spec, spec, spec, P("head"), P("head")),
        out_specs=(spec, spec, spec), check_vma=False)
```

```python
import functools

import jax
import jax.numpy as jnp
from jax import lax
from jax.experimental import pallas as pl
from jax.experimental.pallas import tpu as pltpu
from jax.sharding import PartitionSpec as P

HD = 128
HEADS = 40
BLOCK = 256
epsilon = 1e-05

HALF = HD // 2
F32 = jnp.float32
BF16 = jnp.bfloat16
VMEM = pl.BlockSpec(memory_space=pltpu.VMEM)
HBM = pl.BlockSpec(memory_space=pltpu.HBM)


def dot(a, b, ca, cb):
    return lax.dot_general(a, b, (((ca,), (cb,)), ((), ())), preferred_element_type=F32)


def lanes_of(h):
    return slice(h * HD, (h + 1) * HD)


def head(ref, h):
    return ref[:, lanes_of(h)]


def decay_in_of(rate):
    place = lax.broadcasted_iota(jnp.int32, (8, HD), 0).astype(F32)
    table = jnp.exp(-rate * (place + 1.0))
    while table.shape[0] < BLOCK:
        step = jnp.exp(jnp.full((1, HD), -float(table.shape[0]), F32) * rate)
        table = jnp.concatenate([table, table * step], axis=0)
    return table


def decay_out_of(rate):
    place = lax.broadcasted_iota(jnp.int32, (8, HD), 0).astype(F32)
    table = jnp.exp(-rate * (7.0 - place))
    while table.shape[0] < BLOCK:
        step = jnp.exp(jnp.full((1, HD), -float(table.shape[0]), F32) * rate)
        table = jnp.concatenate([table * step, table], axis=0)
    return table


def mask_of(rates, decay_in):
    row = lax.broadcasted_iota(jnp.int32, (BLOCK, BLOCK), 0)
    col = lax.broadcasted_iota(jnp.int32, (BLOCK, BLOCK), 1)
    place = lax.broadcasted_iota(jnp.int32, (1, BLOCK), 1).astype(F32)
    growth = jnp.exp(rates * (place + 1.0))
    both = jnp.concatenate([decay_in, decay_in], axis=1) * growth
    return jnp.where(row >= col, both, 0.0)


def short(rows, h):
    return rows[h:h + 1, 0:HD]


def scaled(array, scale):
    return (array.astype(F32) * scale).astype(BF16)


def put_halves(keep, send, h, state, odd):
    chips = keep.shape[0]
    share = HD // 2 // chips
    low, high = state[:HD // 2], state[HD // 2:]
    mine, other = jnp.where(odd, high, low), jnp.where(odd, low, high)
    for r in range(share):
        lane = (h * share + r) * HD
        keep[:, lane:lane + HD] = mine[r * chips:(r + 1) * chips]
        send[:, lane:lane + HD] = other[r * chips:(r + 1) * chips]


def put_half(ref, h, state):
    chips = ref.shape[0]
    share = HD // 2 // chips
    for r in range(share):
        lane = (h * share + r) * HD
        ref[:, lane:lane + HD] = state[r * chips:(r + 1) * chips]


def get_half(ref, h):
    chips = ref.shape[0]
    share = HD // 2 // chips
    return jnp.concatenate([ref[:, lanes_of(h * share + r)] for r in range(share)], axis=0)


def rows_of(h, size, start=0):
    return slice(start + h * size, start + (h + 1) * size)


def whole(mine, other, odd):
    low, high = jnp.where(odd, other, mine), jnp.where(odd, mine, other)
    return jnp.concatenate([low, high], axis=0)


def get_state(mine, other, h, odd):
    return whole(get_half(mine, h), get_half(other, h), odd).astype(BF16)


def kv_kernel(rates, keys, values, queries, out_grad, keep, send, rows, mixing, key_in, value_in, query_in, grad_in,
              rate, decays, sems):
    count = rates.shape[0]
    odd = lax.rem(lax.axis_index("ctx"), 2) == 1
    pairs = ((rates, rate), (keys, key_in), (values, value_in), (queries, query_in), (out_grad, grad_in))
    copies = [pltpu.make_async_copy(source, target, sems.at[i]) for i, (source, target) in enumerate(pairs)]
    for copy in copies:
        copy.start()
    copies[0].wait()
    wide = mixing.shape[1] // count
    index = lax.broadcasted_iota(jnp.int32, (8, wide), 0)
    for h in range(count):
        rows[h:h + 1, :] = jnp.full((1, BLOCK), rate[h], F32)
        decay = jnp.exp(jnp.full((8, wide), -rate[h] * BLOCK, F32))
        place = lax.rem(index, 4)
        later = index >= 4
        first = later == odd
        on_first = jnp.where(place == 0, decay, jnp.where(place == 2, 0.0, 1.0))
        on_second = jnp.where(place == 1, decay, jnp.where(place == 3, 0.0, 1.0))
        mixing[:, h * wide:(h + 1) * wide] = jnp.where(first, on_first, on_second)
        decays[:, lanes_of(h)] = decay_out_of(jnp.full((1, HD), rate[h], F32))
    copies[1].wait()
    key_dec = [scaled(head(key_in, h), head(decays, h)) for h in range(count)]
    copies[2].wait()
    for h in range(count):
        put_halves(keep, send, h, dot(head(value_in, h), key_dec[h], 0, 0), odd)
    copies[3].wait()
    copies[4].wait()


def odd_of(mixing, width=HD):
    return mixing[2:3, 0:width] > 0.5


def intra_kernel(rows, mixing, queries, keys, values, out_grad, gain, attn, query_t, intra_t, weighted_t, partner):
    odd = odd_of(mixing, BLOCK)
    count = queries.shape[1] // HD
    for h in range(count):
        decay_in = decay_in_of(short(rows, h))
        scores = dot(head(queries, h), head(keys, h), 1, 1)
        weights = (scores * mask_of(rows[h:h + 1, :], decay_in)).astype(BF16)
        attn[h] = weights
        query_dec = scaled(head(queries, h), decay_in).astype(F32).T
        query_t[rows_of(h, HD), :] = query_dec.astype(BF16)
        partner[rows_of(h, HD), :] = query_dec
        intra = dot(head(values, h), weights, 0, 1)
        weighted = (head(out_grad, h).astype(F32) * head(gain, h)).T
        start = count * HD
        for array, target in ((intra, intra_t), (weighted, weighted_t)):
            low, high = array[:HALF], array[HALF:]
            target[rows_of(h, HALF), :] = jnp.where(odd, high, low)
            partner[rows_of(h, HALF, start), :] = jnp.where(odd, low, high)
            start += count * HALF


def factors(mixing, backward):
    return [mixing[i:i + 1, :] for i in range(4 * backward, 4 * backward + 4)]


def join_kernel(backward, mixing, keep, got, total):
    own, coming = factors(mixing, backward)[:2]
    total[:, 0, :] = own * keep[...] + coming * got[...]


def spread_kernel(backward, mixing, base, prefix, mine, other):
    own, coming, add_mine, add_other = factors(mixing, backward)
    incoming = prefix[:, 0, :]
    other[...] = own * incoming + add_other * base[...]
    mine[...] = coming * incoming + add_mine * base[...]


def scan_kernel(backward, rows, totals, prefix):
    chips, one, width = totals.shape
    count = width * chips * 2 // HD // HD
    wide = width // count
    row = lax.broadcasted_iota(jnp.int32, (chips, chips), 0)
    col = lax.broadcasted_iota(jnp.int32, (chips, chips), 1)
    far = ((col - row - 1) if backward else (row - col - 1)).astype(F32)
    for h in range(count):
        lanes = slice(h * wide, (h + 1) * wide)
        rate = rows[h:h + 1, 0:chips]
        weight = jnp.where(far >= 0.0, jnp.exp(-(rate * (2.0 * BLOCK)) * jnp.maximum(far, 0.0)), 0.0)
        prefix[:, 0, lanes] = lax.dot_general(
            weight, totals[:, 0, lanes], (((1,), (0,)), ((), ())),
            precision=lax.Precision.HIGHEST, preferred_element_type=F32)


def fold(array):
    return jnp.sum(array.reshape(HALF // 8, 8, BLOCK), axis=0)


def blocks_of(h, count, query_t, intra_t, weighted_t, partner):
    mine = (query_t[rows_of(h, HD), :], intra_t[rows_of(h, HALF), :], weighted_t[rows_of(h, HALF), :])
    other = (partner[rows_of(h, HD), :].astype(BF16), partner[rows_of(h, HALF, count * HD), :],
             partner[rows_of(h, HALF, count * (HD + HALF)), :])
    return mine, other


def out_kernel(mixing, keep, got, prefix, query_t, intra_t, weighted_t, partner, out, held, sums):
    chips, width = keep.shape
    count = query_t.shape[0] // HD
    wide = width // count
    share = wide // HD
    sums_of = [[jnp.zeros((8, BLOCK), F32) for _ in range(2)] for _ in range(2)]
    for h in range(count):
        own, coming, add_mine, add_other = (row[:, h * wide:h * wide + HD] for row in factors(mixing, False))
        incoming = jnp.concatenate([prefix[:, 0, lanes_of(h * share + r)] for r in range(share)], axis=0)
        states = (coming * incoming + add_mine * get_half(got, h), own * incoming + add_other * get_half(keep, h))
        for which, (query, intra, weighted) in enumerate(blocks_of(h, count, query_t, intra_t, weighted_t, partner)):
            state = states[which].astype(BF16)
            held[which, rows_of(h, HALF), :] = state.astype(F32)
            result = intra + dot(state, query, 1, 0)
            out[which, rows_of(h, HALF), :] = result
            sums_of[which][0] = sums_of[which][0] + fold(result * result)
            sums_of[which][1] = sums_of[which][1] + fold(weighted * result)
    odd = odd_of(mixing, BLOCK)
    mine, other = ([jnp.sum(part, axis=0, keepdims=True) for part in parts] for parts in sums_of)
    even_block = [jnp.where(odd, b, a) for a, b in zip(mine, other)]
    odd_block = [jnp.where(odd, a, b) for a, b in zip(mine, other)]
    both = jnp.concatenate(even_block + odd_block, axis=0)
    for peer in range(sums.shape[0]):
        sums[peer] = both


def pack_kernel(grad_t, held, exchange):
    exchange[:, 0:BLOCK] = grad_t[1].astype(F32)
    exchange[:, BLOCK:BLOCK + HD] = held[1]


def grad_kernel(mixing, sums, out, query_t, intra_t, weighted_t, partner, total, base, grad_t):
    odd = odd_of(mixing, BLOCK)
    count = query_t.shape[0] // HD
    first = mixing[7:8, 0:HD] > 0.5
    chips, one, width = total.shape
    wide = width // count
    share = wide // HD
    summed = jnp.sum(sums[...], axis=0)
    even_block, odd_block = summed[0:2], summed[2:4]
    scales = []
    for block in (jnp.where(odd, odd_block, even_block), jnp.where(odd, even_block, odd_block)):
        inverse = lax.rsqrt(block[0:1] / (HEADS * HD) + epsilon)
        scales.append((inverse, inverse * inverse * inverse * block[1:2] / (HEADS * HD)))
    for h in range(count):
        own, coming = (row[:, h * wide:h * wide + HD] for row in factors(mixing, True)[:2])
        terms = []
        for which, (query, intra, weighted) in enumerate(blocks_of(h, count, query_t, intra_t, weighted_t, partner)):
            inverse, factor = scales[which]
            grad = (weighted * inverse - out[which, rows_of(h, HALF), :] * factor).astype(BF16)
            grad_t[which, rows_of(h, HALF), :] = grad
            terms.append(dot(grad, query, 1, 1))
        put_half(base, h, jnp.where(first, terms[0], terms[1]))
        joined = own * terms[0] + coming * terms[1]
        for r in range(share):
            total[:, 0, lanes_of(h * share + r)] = joined[r * chips:(r + 1) * chips]


def local_kernel(rows, mixing, keys, values, grad_t, held, exchange, query_grad, back_attn, whole_grad):
    for h in range(keys.shape[1] // HD):
        place = lax.broadcasted_iota(jnp.int32, (1, BLOCK), 1).astype(F32)
        grad = whole(grad_t[0, rows_of(h, HALF), :].astype(F32), exchange[rows_of(h, HALF), 0:BLOCK], odd_of(mixing, BLOCK))
        state = whole(held[0, rows_of(h, HALF), :], exchange[rows_of(h, HALF), BLOCK:BLOCK + HD], odd_of(mixing))
        grad_dec = (grad * jnp.exp(-rows[h:h + 1, :] * (place + 1.0))).astype(BF16)
        grad = grad.astype(BF16)
        whole_grad[rows_of(h, HD), :] = grad
        mask = mask_of(rows[h:h + 1, :], decay_in_of(short(rows, h)))
        back = (dot(grad, head(values, h), 0, 1) * mask).astype(BF16)
        back_attn[h] = back
        query_grad[:, lanes_of(h)] = (
            dot(back, head(keys, h), 1, 0) + dot(grad_dec, state.astype(BF16), 0, 0)).astype(BF16)


def parts_kernel(queries, attn, back_attn, whole_grad, key_part, value_part):
    for h in range(attn.shape[0]):
        key_part[:, lanes_of(h)] = dot(back_attn[h], head(queries, h), 0, 0)
        value_part[:, lanes_of(h)] = dot(attn[h], whole_grad[rows_of(h, HD), :], 0, 1)


def last_kernel(rows, mixing, keys, values, mine, other, key_part, value_part, query_out,
                query_grad, key_grad, value_grad, key_out, value_out, sems):
    odd = odd_of(mixing)
    copies = [pltpu.make_async_copy(query_out, query_grad, sems.at[2 * (keys.shape[1] // HD)])]
    copies[0].start()
    for h in range(keys.shape[1] // HD):
        later = get_state(mine, other, h, odd)
        decay_out = decay_out_of(short(rows, h))
        value_dec = scaled(head(values, h), decay_out)
        key_dec = scaled(head(keys, h), decay_out)
        key_out[:, lanes_of(h)] = (head(key_part, h) + dot(value_dec, later, 1, 0)).astype(BF16)
        value_out[:, lanes_of(h)] = (head(value_part, h) + dot(key_dec, later, 1, 1)).astype(BF16)
        if h % 2 == 0 and h + 1 < keys.shape[1] // HD:
            continue
        lanes = slice((h - h % 2) * HD, (h + 1) * HD)
        for which, (source, target) in enumerate(((key_out, key_grad), (value_out, value_grad))):
            copies.append(pltpu.make_async_copy(
                source.at[:, lanes], target.at[:, lanes], sems.at[2 * h + which]))
            copies[-1].start()
    for copy in copies:
        copy.wait()


def call(body, name, args, shapes, specs=None, scratch=(), flops=0, into=VMEM):
    outs = [jax.ShapeDtypeStruct(shape, kind) for shape, kind in shapes]
    moved = sum(a.size * a.dtype.itemsize for a in args)
    return pl.pallas_call(
        body,
        out_shape=outs if len(outs) > 1 else outs[0],
        in_specs=specs or [VMEM] * len(args),
        out_specs=[into] * len(outs) if len(outs) > 1 else into,
        scratch_shapes=list(scratch),
        compiler_params=pltpu.CompilerParams(vmem_limit_bytes=16 * 1024 * 1024),
        cost_estimate=pl.CostEstimate(flops=flops, bytes_accessed=moved, transcendentals=0),
        name=name,
    )(*args)


def per_device(queries, keys, values, out_grad, rates, gain):
    tokens, width = queries.shape
    count = rates.shape[0]
    chips = lax.axis_size("ctx") // 2
    ranks = lax.axis_size("head")
    lanes = count * HD * HALF // chips
    half, flat, rows_half = ((chips, lanes), F32), ((chips, 1, lanes), F32), ((count * HALF, BLOCK), F32)
    gain = gain.reshape(1, width)
    wide16, wide32 = ((BLOCK, width), BF16), ((BLOCK, width), F32)
    square = ((count, BLOCK, BLOCK), BF16)
    unit = BLOCK * BLOCK * width
    partners = [(i, i ^ 1) for i in range(2 * chips)]
    rings = [[2 * i + c for i in range(chips)] for c in range(2)]
    towers = [[(2 * i + c) * ranks + y for c in range(2) for y in range(ranks)] for i in range(chips)]

    def swap(array):
        return lax.ppermute(array, "ctx", partners)

    def spread_out(array):
        return lax.all_to_all(array, "ctx", 0, 0, tiled=True, axis_index_groups=rings)

    keep, send, rows, mixing, key_in, value_in, query_in, grad_in = call(
        kv_kernel, "kv", [pltpu.with_memory_space_constraint(a, pltpu.HBM) for a in (rates, keys, values, queries, out_grad)],
        [half, half, ((8, BLOCK), F32), ((8, lanes), F32)] + [wide16] * 4,
        specs=[HBM] * 5,
        scratch=[pltpu.SMEM((count,), F32), pltpu.VMEM((BLOCK, width), F32),
                 pltpu.SemaphoreType.DMA((5,))])
    got = swap(send)
    attn, query_t, intra_t, weighted_t, partner = call(
        intra_kernel, "intra", [rows, mixing, query_in, key_in, value_in, grad_in, gain],
        [square, ((width, BLOCK), BF16), rows_half, rows_half, ((2 * width, BLOCK), F32)], flops=4 * unit)
    got, partner = lax.optimization_barrier((got, partner))
    total = call(functools.partial(join_kernel, False), "join", [mixing, keep, got], [flat])
    total, partner = lax.optimization_barrier((total, partner))
    partner = swap(partner)
    total = spread_out(total)
    prefix = spread_out(call(functools.partial(scan_kernel, False), "scan", [rows, total], [flat]))
    shared = [query_t, intra_t, weighted_t, partner]
    out, held, sums = call(
        out_kernel, "out", [mixing, keep, got, prefix] + shared,
        [((2, count * HALF, BLOCK), F32), ((2, count * HALF, HD), F32), ((2 * ranks, 4, BLOCK), F32)])
    sums = lax.all_to_all(sums, ("ctx", "head"), 0, 0, tiled=True, axis_index_groups=towers)
    total, base, grad_t = call(
        grad_kernel, "grad", [mixing, sums, out] + shared,
        [flat, half, ((2, count * HALF, BLOCK), BF16)])
    total = spread_out(total)
    exchange = swap(call(pack_kernel, "pack", [grad_t, held], [((count * HALF, BLOCK + HD), F32)], flops=4 * unit))
    prefix = spread_out(call(functools.partial(scan_kernel, True), "scan", [rows, total], [flat]))
    mine, other = call(
        functools.partial(spread_kernel, True), "spread", [mixing, base, prefix], [half, half])
    tied, other = lax.optimization_barrier((rows, other))
    other = swap(other)
    query_grad, back_attn, whole_grad = call(
        local_kernel, "local", [tied, mixing, keys, values, grad_t, held, exchange],
        [wide16, square, ((width, BLOCK), BF16)], flops=4 * unit)
    key_part, value_part = call(
        parts_kernel, "parts", [queries, attn, back_attn, whole_grad], [wide32, wide32], flops=4 * unit)
    other, key_part, value_part = lax.optimization_barrier((other, key_part, value_part))
    outs = call(
        last_kernel, "last", [rows, mixing, keys, values, mine, other, key_part, value_part, query_grad],
        [wide16] * 3,
        scratch=[pltpu.VMEM((BLOCK, width), BF16), pltpu.VMEM((BLOCK, width), BF16),
                 pltpu.SemaphoreType.DMA((2 * count + 1,))],
        into=HBM)
    return tuple(outs)


def solution(mesh):
    spec = P("ctx", "head")
    return jax.shard_map(
        per_device, mesh=mesh, in_specs=(spec, spec, spec, spec, P("head"), P("head")),
        out_specs=(spec, spec, spec), check_vma=False)
```
